256 devices in a mesh: gx: 8 (over x, y_hi), gy: 16 (over z, core), gz: 2 (over y_lo).
Axes of the slice: x: 4, y: 4 (y_hi: 2, y_lo: 2; y = y_hi * 2 + y_lo), z: 8, core: 2. Of those that a mesh axis runs over, the one named last changes fastest.
Arguments:
- populations: float32 [27, 64, 128, 256], P(None, 'gx', 'gy', 'gz'), may hold values from 0.5 to 1.5
- soot_moments: float32 [6, 64, 128, 256], P(None, 'gx', 'gy', 'gz'), may hold values from 0.2 to 2
- growth_rate: float32 [64, 128, 256], P('gx', 'gy', 'gz'), may hold values from 0 to 0.3
- moment_rates: float32 [27], replicated, may hold values from 0.5 to 1.95
Outputs:
- next_populations: float32 [27, 64, 128, 256], P(None, 'gx', 'gy', 'gz')
- next_soot: float32 [6, 64, 128, 256], P(None, 'gx', 'gy', 'gz')
The draws below stay inside these ranges and needn't reach their ends.
All inputs are finite; a program needn't handle non-finite values.
Results may differ from the reference program's by a relative error of at most 0.0001.
Values sent between devices are 32-bit elements; how exact they have to be, the bound alone decides.
A program may use at most 128 MiB of HBM per device.

```python
import math
import jax
import jax.numpy as jnp
import numpy as np
from jax import lax

STEPS = 2
NX = 64
NY = 128
NZ = 256


def level_of(key, dims, split, smallest, largest):
    factor_of = 1.0
    for axis_at, blocks in split:
        steps = jax.random.uniform(jax.random.fold_in(jax.random.fold_in(key, 6), axis_at), (blocks,), jnp.float32, smallest / len(split), largest / len(split))
        factor_of = factor_of * jnp.repeat(jnp.exp(steps), dims[axis_at] // blocks).reshape((-1,) + (1,) * (len(dims) - 1 - axis_at))
    return factor_of


def setup_inputs(seed: int = 0) -> dict:
    seeds = jax.random.split(jax.random.key(seed), 5)
    return {
        "populations": jnp.clip(0.5 + 1.0 * jax.random.uniform(seeds[0], (27, NX, NY, NZ), jnp.float32) ** level_of(seeds[0], (27, NX, NY, NZ), ((1, 8), (2, 16), (3, 2)), -0.2, 0.2), 0.5, 1.5),
        "soot_moments": jnp.clip(jnp.exp(math.log(2.0) - 2.3025851 * jax.random.uniform(seeds[1], (6, NX, NY, NZ), jnp.float32) ** level_of(seeds[1], (6, NX, NY, NZ), ((1, 8), (2, 16), (3, 2)), -0.2, 0.2)), 0.2, 2.0),
        "growth_rate": jnp.clip(0.3 * jax.random.uniform(seeds[2], (NX, NY, NZ), jnp.float32) ** level_of(seeds[2], (NX, NY, NZ), ((0, 8), (1, 16), (2, 2)), -0.2, 0.2), 0.0, 0.3),
        "moment_rates": jnp.clip(jax.random.uniform(seeds[3], (27,), jnp.float32, 0.5, 1.95), 0.5, 1.95),
    }


highest = lax.Precision.HIGHEST
diffusivity = (0.08, 0.06, 0.05, 0.04, 0.035, 0.03)
offsets = (0, 1, -1)


def velocity_of(index):
    return (offsets[index // 9], offsets[index // 3 % 3], offsets[index % 3])


def lattice_tables():
    speeds = np.array([0.0, 1.0, -1.0])
    single = np.array([2.0 / 3.0, 1.0 / 6.0, 1.0 / 6.0])
    powers = np.array([[1.0, 1.0, 1.0], [0.0, 1.0, -1.0], [0.0, 1.0, 1.0]])
    undo_powers = np.array([[1.0, 0.0, -1.0], [0.0, 0.5, 0.5], [0.0, -0.5, 0.5]])
    weights = np.kron(np.kron(single, single), single)
    lattice = np.stack(np.meshgrid(speeds, speeds, speeds, indexing="ij"), 0).reshape(3, 27)
    forward = np.kron(np.kron(powers, powers), powers) * weights[None, :]
    backward = np.kron(np.kron(undo_powers, undo_powers), undo_powers) / weights[:, None]
    moment_rows = np.concatenate([weights[None, :], weights[None, :] * lattice], 0)
    return (jnp.asarray(forward, jnp.float32), jnp.asarray(backward, jnp.float32),
            jnp.asarray(lattice.T, jnp.float32), jnp.asarray(moment_rows, jnp.float32))


def macroscopic(populations, moment_rows):
    flat = populations.reshape(27, -1)
    totals = jnp.dot(moment_rows, flat, precision=highest)
    return totals.reshape((4,) + populations.shape[1:])


def collide(populations, moment_sums, relaxation, lattice):
    density = moment_sums[0]
    velocity = moment_sums[1:4]
    projected = jnp.tensordot(lattice, velocity, axes=1, precision=highest)
    squared = jnp.sum(velocity * velocity, axis=0)
    balance = density[None] + 3.0 * projected + 4.5 * projected * projected - 1.5 * squared[None]
    departure = (populations - balance).reshape(27, -1)
    return populations - jnp.dot(relaxation, departure, precision=highest).reshape(populations.shape)


def soot_reference(soot_fields, velocity, growth_rate):
    kappa = jnp.asarray(diffusivity, jnp.float32)[:, None, None, None]
    advected = jnp.zeros_like(soot_fields)
    neighbours = jnp.zeros_like(soot_fields)
    for spatial_dim in range(3):
        flux = velocity[spatial_dim][None] * soot_fields
        advected = advected + (jnp.roll(flux, -1, spatial_dim + 1) - jnp.roll(flux, 1, spatial_dim + 1))
        neighbours = neighbours + (jnp.roll(soot_fields, -1, spatial_dim + 1) + jnp.roll(soot_fields, 1, spatial_dim + 1))
    laplacian = neighbours - 6.0 * soot_fields
    return soot_fields - 0.5 * advected + kappa * laplacian + growth_rate[None] * soot_fields


def propagate_reference(collided):
    pieces = []
    for index in range(27):
        pieces.append(jnp.roll(collided[index], velocity_of(index), axis=(0, 1, 2)))
    return jnp.stack(pieces, 0)


def reference(populations, soot_moments, growth_rate, moment_rates):
    forward, backward, lattice, moment_rows = lattice_tables()
    relaxation = jnp.dot(backward * moment_rates[None, :], forward, precision=highest)
    soot_fields = soot_moments
    for repeat in range(STEPS):
        moment_sums = macroscopic(populations, moment_rows)
        soot_fields = soot_reference(soot_fields, moment_sums[1:4], growth_rate)
        collided = collide(populations, moment_sums, relaxation, lattice)
        populations = propagate_reference(collided)
    return populations, soot_fields
```

```python
import functools

import jax
import jax.numpy as jnp
from jax import lax
from jax.experimental import pallas as pl
from jax.experimental.pallas import tpu as pltpu
from jax.sharding import PartitionSpec as P

MESH = pl.DeviceIdType.MESH
STEPS = 2
KAPPA = (0.08, 0.06, 0.05, 0.04, 0.035, 0.03)
SPEED = (0, 1, -1)
LAST = 127
SIDES = (1, 2)
CORNERS = ((1, 1), (1, 2), (2, 1), (2, 2))
SOOT = {(0, 1): 18, (0, 2): 33, (1, 1): 39, (1, 2): 45, (2, 1): 51, (2, 2): 57}
FIELDS = 63
ROWS = 168
X, XZ, XY, XYZ, Y, YZ, Z = 0, 2, 4, 8, 12, 14, 16
MESSAGES = 17


def pop(a, b, e):
    return (0, 9, 24)[a] + 3 * b + e


def block(slot):
    return 16 * slot + 8


def forward(f):
    total = f[1] + f[2]
    return (4.0 * f[0] + total, f[1] - f[2], total)


def backward(n):
    return (0.5 * (n[0] - n[2]), n[1] + n[2], n[2] - n[1])


def along(values, axis, change):
    out = {}
    for i in range(3):
        for j in range(3):
            keys = [(i, j)[:axis] + (k,) + (i, j)[axis:] for k in range(3)]
            for key, value in zip(keys, change([values[key] for key in keys])):
                out[key] = value
    return out


def moment_constants(rates_ref, consts):
    for index in range(27):
        powers = (index // 9, index // 3 % 3, index % 3)
        rate = rates_ref[index]
        consts[index] = 0.125 - 0.125 * rate
        consts[27 + index] = rate * (27.0 / 3.0 ** powers.count(2))


def collide(g, consts):
    m = g
    for axis in (2, 1, 0):
        m = along(m, axis, forward)
    scale = 1.0 / 216.0
    density = m[0, 0, 0] * scale
    u = (m[1, 0, 0] * scale, m[0, 1, 0] * scale, m[0, 0, 1] * scale)
    square = [3.0 * v * v for v in u]
    product = {(0, 1): u[0] * u[1], (0, 2): u[0] * u[2], (1, 2): u[1] * u[2]}
    n = {}
    for key, value in m.items():
        index = 9 * key[0] + 3 * key[1] + key[2]
        odd = tuple(i for i in range(3) if key[i] == 1)
        part = consts[index] * value
        if len(odd) == 3:
            n[key] = part
            continue
        if len(odd) == 0:
            balance = density
            for i in range(3):
                if key[i] == 2:
                    balance = balance + square[i]
        elif len(odd) == 1:
            balance = u[odd[0]]
        else:
            balance = product[odd]
        n[key] = part + consts[27 + index] * balance
    for axis in (0, 1, 2):
        n = along(n, axis, backward)
    return n, u


def turn(value, e):
    return value if e == 0 else pltpu.roll(value, 1 if e == 1 else LAST, 1)


def lane_of(e):
    return 0 if e == 1 else LAST


def layer_out(x, g, soot, growth, consts, F, center, faces, zs):
    lane = lax.broadcasted_iota(jnp.int32, (8, 128), 1)
    base = pl.multiple_of(16 * x + 24, 8)

    def put(field, value):
        F[field, pl.ds(base, 8), :] = value
        if faces is not None:
            side, buffer = faces
            first = 9 if side == 1 else 24
            if first <= field < first + 15:
                buffer[side - 1, field - first] = value

    n, u = collide(g, consts)
    packed = {1: None, 2: None}

    def pack(e, place, value):
        moved = pltpu.roll(value, (8 * place - lane_of(e)) % 128, 1)
        packed[e] = moved if packed[e] is None else jnp.where(lane == 8 * place, moved, packed[e])

    for a in range(3):
        for b in range(3):
            for e in range(3):
                value = turn(n[a, b, e], e)
                put(pop(a, b, e), value)
                if e:
                    pack(e, 3 * a + b, value)
    half = [0.5 * v for v in u]
    for j in range(6):
        for axis in range(3):
            plus = soot[j] * (KAPPA[j] + half[axis])
            minus = soot[j] * (KAPPA[j] - half[axis])
            if axis == 2:
                plus, minus = turn(plus, 1), turn(minus, 2)
                pack(1, 9 + j, plus)
                pack(2, 9 + j, minus)
            put(SOOT[axis, 1] + j, plus)
            put(SOOT[axis, 2] + j, minus)
        center[j, x] = soot[j] * (growth + (1.0 - 6.0 * KAPPA[j]))
    for e in SIDES:
        moved = pltpu.roll(packed[e], x, 1)
        zs[e - 1] = jnp.where(lax.rem(lane, 8) == x, moved, zs[e - 1])


def pull(F, center, x):
    g = {}
    for a in range(3):
        for b in range(3):
            for e in range(3):
                g[a, b, e] = F[pop(a, b, e), pl.ds(16 * (x - SPEED[a]) + 24 - SPEED[b], 8), :]
    soot = []
    for j in range(6):
        total = center[j, x]
        for axis in range(3):
            for side in SIDES:
                move = (16, 1, 0)[axis] * SPEED[side]
                total = total + F[SOOT[axis, side] + j, pl.ds(16 * x + 24 - move, 8), :]
        soot.append(total)
    return g, soot


def kernel(
    pops_ref, soot_ref, growth_ref, rates_ref, pops_out, soot_out,
    G, S, R, F0, F1, C0, C1, xs, xzs, xzh, xys, xyh, xyzh, ys, yh, yzs, yzh, zs, zh, consts, load_sem, send_sem, recv_sem,
):
    position = tuple(lax.axis_index(axis) for axis in ("gx", "gy", "gz"))
    counts = tuple(lax.axis_size(axis) for axis in ("gx", "gy", "gz"))

    def device(*move):
        return tuple(lax.rem(p + (m + n), n) for p, m, n in zip(position, move, counts))

    targets = [(i, j, k) for i in (0, 1, -1) for j in (0, 1, -1) for k in (0, 1) if (i, j, k) != (0, 0, 0)]
    barrier = pltpu.get_barrier_semaphore()
    for target in sorted(targets, key=lambda t: -abs(t[0])):
        pl.semaphore_signal(barrier, inc=1, device_id=device(*target), device_id_type=MESH)

    loads = [
        pltpu.make_async_copy(source, target, load_sem.at[i])
        for i, (source, target) in enumerate(
            [
                (pops_ref.at[:, 0:1], G.at[:, 0:1]),
                (pops_ref.at[:, 7:8], G.at[:, 7:8]),
                (soot_ref, S),
                (growth_ref, R),
                (pops_ref.at[:, 1:7], G.at[:, 1:7]),
            ]
        )
    ]
    for load in loads:
        load.start()
    moment_constants(rates_ref, consts)
    zs[...] = jnp.zeros_like(zs)
    xys[...] = jnp.zeros_like(xys)

    F, C = (F0, F1), (C0, C1)
    lane = lax.broadcasted_iota(jnp.int32, (8, 128), 1)
    sublane = lax.broadcasted_iota(jnp.int32, (8, 128), 0)

    def message(step, index, source, target, move):
        return pltpu.make_async_remote_copy(
            src_ref=source,
            dst_ref=target,
            send_sem=send_sem.at[step, index],
            recv_sem=recv_sem.at[step, index],
            device_id=device(*move),
            device_id_type=MESH,
        )

    def messages(step):
        out = [None] * MESSAGES
        for a in SIDES:
            first, slot = (9, 0) if a == 1 else (24, 9)
            out[X + a - 1] = message(
                step, X + a - 1, xs.at[step, a - 1], F[step].at[pl.ds(first, 15), pl.ds(block(slot), 8)], (SPEED[a], 0, 0)
            )
            out[XZ + a - 1] = message(
                step, XZ + a - 1, xzs.at[step, a - 1], xzh.at[step, a - 1], (SPEED[a], 0, 1)
            )
            out[Y + a - 1] = message(step, Y + a - 1, ys.at[step, a - 1], yh.at[step, a - 1], (0, SPEED[a], 0))
            out[YZ + a - 1] = message(step, YZ + a - 1, yzs.at[step, a - 1], yzh.at[step, a - 1], (0, SPEED[a], 1))
        for d, (a, b) in enumerate(CORNERS):
            out[XY + d] = message(step, XY + d, xys.at[step, d], xyh.at[step, d], (SPEED[a], SPEED[b], 0))
            out[XYZ + d] = message(step, XYZ + d, xys.at[step, d], xyzh.at[step, d], (SPEED[a], SPEED[b], 1))
        out[Z] = message(step, Z, zs.at[step], zh.at[step], (0, 0, 1))
        return out

    sent = [messages(step) for step in range(STEPS)]

    def pack_x(step):
        for a in SIDES:
            slot = 8 if a == 1 else 1
            packed = None
            for b in range(3):
                for e in SIDES:
                    place = 3 * (e - 1) + b
                    moved = pltpu.roll(F[step][pop(a, b, e), block(slot) : block(slot) + 8, :], (place - lane_of(e)) % 128, 1)
                    packed = moved if packed is None else jnp.where(lane == place, moved, packed)
            xzs[step, a - 1] = packed
        for d, (a, b) in enumerate(CORNERS):
            row = block(8 if a == 1 else 1) + (7 if b == 1 else 0)
            for e in range(3):
                xys[step, d, e : e + 1, :] = F[step][pop(a, b, e), row : row + 1, :]

    def pack_y(step):
        for b in SIDES:
            row = block(1) + (7 if b == 1 else 0)
            packed = None
            for a in range(3):
                for e in range(3):
                    value = F[step][pop(a, b, e), pl.ds(row, 8, stride=16), :]
                    ys[step, b - 1, 3 * a + e] = value
                    if e:
                        place = 3 * (e - 1) + a
                        moved = pltpu.roll(value, (place - lane_of(e)) % 128, 1)
                        packed = moved if packed is None else jnp.where(lane == place, moved, packed)
            yzs[step, b - 1] = packed
            for j in range(6):
                ys[step, b - 1, 9 + j] = F[step][SOOT[1, b] + j, pl.ds(row, 8, stride=16), :]

    def fix_yz(step):
        for i in (Z, Y, Y + 1, YZ, YZ + 1):
            sent[step][i].wait_recv()

        def fix_layer(x, carry):
            base = pl.multiple_of(16 * x + 24, 8)
            for e in SIDES:
                packed = pltpu.roll(zh[step, e - 1], lax.rem(128 - x, 128), 1)
                for place in range(15):
                    field = pop(place // 3, place % 3, e) if place < 9 else SOOT[2, e] + place - 9
                    moved = pltpu.roll(packed, (lane_of(e) - 8 * place) % 128, 1)
                    pltpu.store(F[step].at[field, pl.ds(base, 8), :], moved, mask=lane == lane_of(e))
            return carry

        lax.fori_loop(0, 8, fix_layer, 0)
        for b in SIDES:
            row = block(1) + (-1 if b == 1 else 8)
            packed = yzh[step, b - 1]
            for a in range(3):
                for e in range(3):
                    value = yh[step, b - 1, 3 * a + e]
                    if e:
                        place = 3 * (e - 1) + a
                        moved = pltpu.roll(packed, (lane_of(e) - place) % 128, 1)
                        value = jnp.where(lane == lane_of(e), moved, value)
                    F[step][pop(a, b, e), pl.ds(row, 8, stride=16), :] = value
            for j in range(6):
                F[step][SOOT[1, b] + j, pl.ds(row, 8, stride=16), :] = yh[step, b - 1, 9 + j]

    def fix_x(step):
        for i in list(range(X, Y)):
            sent[step][i].wait_recv()
        for a in SIDES:
            slot = 0 if a == 1 else 9
            packed = xzh[step, a - 1]
            for b in range(3):
                for e in SIDES:
                    place = 3 * (e - 1) + b
                    moved = pltpu.roll(packed, (lane_of(e) - place) % 128, 1)
                    pltpu.store(
                        F[step].at[pop(a, b, e), block(slot) : block(slot) + 8, :], moved, mask=lane == lane_of(e)
                    )
        other = ((sublane == 1) & (lane == 0)) | ((sublane == 2) & (lane == LAST))
        for d, (a, b) in enumerate(CORNERS):
            row = block(0 if a == 1 else 9) + (-1 if b == 1 else 8)
            value = jnp.where(other, xyzh[step, d], xyh[step, d])
            for e in range(3):
                F[step][pop(a, b, e), row : row + 1, :] = value[e : e + 1, :]

    def given(x):
        g = {(k // 9, k // 3 % 3, k % 3): G[k, x] for k in range(27)}
        return g, [S[j, x] for j in range(6)]

    def layer(step, x, side):
        g, soot = given(x) if step == 0 else pull(F[step - 1], C[step - 1], x)
        faces = None if side is None else (side, xs.at[step])
        layer_out(x, g, soot, R[x], consts, F[step], C[step], faces, zs.at[step])

    def result(x):
        g, soot = pull(F[STEPS - 1], C[STEPS - 1], x)
        for (a, b, e), value in g.items():
            pops_out[9 * a + 3 * b + e, x] = value
        for j in range(6):
            soot_out[j, x] = soot[j]

    def inner(body):
        def step_of(x, carry):
            body(x)
            return carry

        lax.fori_loop(1, 7, step_of, 0)

    for load in loads[:4]:
        load.wait()
    for step in range(STEPS):
        if step > 0:
            fix_yz(step - 1)
            inner(functools.partial(layer, step, side=None))
            fix_x(step - 1)
        layer(step, 0, 2)
        layer(step, 7, 1)
        pack_x(step)
        if step == 0:
            pl.semaphore_wait(barrier, len(targets))
        for i in range(X, Y):
            sent[step][i].start()
        if step == 0:
            loads[4].wait()
            inner(functools.partial(layer, step, side=None))
        pack_y(step)
        for i in (Y, Y + 1, YZ, YZ + 1, Z):
            sent[step][i].start()
    fix_yz(STEPS - 1)
    inner(result)
    fix_x(STEPS - 1)
    result(0)
    result(7)
    for step in range(STEPS):
        for copy in sent[step]:
            copy.wait_send()


def shards(populations, soot_moments, growth_rate, moment_rates):
    f32 = jnp.float32
    hbm = pl.BlockSpec(memory_space=pltpu.HBM)
    vmem = pl.BlockSpec(memory_space=pltpu.VMEM)
    return pl.pallas_call(
        kernel,
        out_shape=(pltpu.VMEM(populations.shape, f32), pltpu.VMEM(soot_moments.shape, f32)),
        in_specs=[hbm, hbm, hbm, pl.BlockSpec(memory_space=pltpu.SMEM)],
        out_specs=(vmem, vmem),
        scratch_shapes=[
            pltpu.VMEM(populations.shape, f32),
            pltpu.VMEM(soot_moments.shape, f32),
            pltpu.VMEM(growth_rate.shape, f32),
            pltpu.VMEM((FIELDS, ROWS, 128), f32),
            pltpu.VMEM((FIELDS, ROWS, 128), f32),
            pltpu.VMEM(soot_moments.shape, f32),
            pltpu.VMEM(soot_moments.shape, f32),
            pltpu.VMEM((STEPS, 2, 15, 8, 128), f32),
            pltpu.VMEM((STEPS, 2, 8, 128), f32),
            pltpu.VMEM((STEPS, 2, 8, 128), f32),
            pltpu.VMEM((STEPS, 4, 8, 128), f32),
            pltpu.VMEM((STEPS, 4, 8, 128), f32),
            pltpu.VMEM((STEPS, 4, 8, 128), f32),
            pltpu.VMEM((STEPS, 2, 15, 8, 128), f32),
            pltpu.VMEM((STEPS, 2, 15, 8, 128), f32),
            pltpu.VMEM((STEPS, 2, 8, 128), f32),
            pltpu.VMEM((STEPS, 2, 8, 128), f32),
            pltpu.VMEM((STEPS, 2, 8, 128), f32),
            pltpu.VMEM((STEPS, 2, 8, 128), f32),
            pltpu.SMEM((54,), f32),
            pltpu.SemaphoreType.DMA((5,)),
            pltpu.SemaphoreType.DMA((STEPS, MESSAGES)),
            pltpu.SemaphoreType.DMA((STEPS, MESSAGES)),
        ],
        compiler_params=pltpu.CompilerParams(
            collective_id=0, has_side_effects=True, vmem_limit_bytes=48 * 1024 * 1024
        ),
    )(populations, soot_moments, growth_rate, moment_rates)


def solution(mesh):
    in_specs = (P(None, "gx", "gy", "gz"), P(None, "gx", "gy", "gz"), P("gx", "gy", "gz"), P())
    out_specs = (P(None, "gx", "gy", "gz"), P(None, "gx", "gy", "gz"))
    return jax.shard_map(shards, mesh=mesh, in_specs=in_specs, out_specs=out_specs, check_vma=False)
```

```python
import functools

import jax
import jax.numpy as jnp
from jax import lax
from jax.experimental import pallas as pl
from jax.experimental.pallas import tpu as pltpu
from jax.sharding import PartitionSpec as P

MESH = pl.DeviceIdType.MESH
STEPS = 2
KAPPA = (0.08, 0.06, 0.05, 0.04, 0.035, 0.03)
SPEED = (0, 1, -1)
LAST = 127
SIDES = (1, 2)
CORNERS = ((1, 1), (1, 2), (2, 1), (2, 2))
SOOT = {(0, 1): 18, (0, 2): 33, (1, 1): 39, (1, 2): 45, (2, 1): 51, (2, 2): 57}
FIELDS = 63
ROWS = 168
X, XZ, XY, XYZ, Y, YZ, Z = 0, 2, 4, 8, 12, 14, 16
MESSAGES = 17


def pop(a, b, e):
    return (0, 9, 24)[a] + 3 * b + e


def block(slot):
    return 16 * slot + 8


def forward(f):
    total = f[1] + f[2]
    return (4.0 * f[0] + total, f[1] - f[2], total)


def backward(n):
    return (0.5 * (n[0] - n[2]), n[1] + n[2], n[2] - n[1])


def along(values, axis, change):
    out = {}
    for i in range(3):
        for j in range(3):
            keys = [(i, j)[:axis] + (k,) + (i, j)[axis:] for k in range(3)]
            for key, value in zip(keys, change([values[key] for key in keys])):
                out[key] = value
    return out


def moment_constants(rates_ref, consts):
    for index in range(27):
        powers = (index // 9, index // 3 % 3, index % 3)
        rate = rates_ref[index]
        consts[index] = 0.125 - 0.125 * rate
        consts[27 + index] = rate * (27.0 / 3.0 ** powers.count(2))


def collide(g, consts):
    m = g
    for axis in (2, 1, 0):
        m = along(m, axis, forward)
    scale = 1.0 / 216.0
    density = m[0, 0, 0] * scale
    u = (m[1, 0, 0] * scale, m[0, 1, 0] * scale, m[0, 0, 1] * scale)
    square = [3.0 * v * v for v in u]
    product = {(0, 1): u[0] * u[1], (0, 2): u[0] * u[2], (1, 2): u[1] * u[2]}
    n = {}
    for key, value in m.items():
        index = 9 * key[0] + 3 * key[1] + key[2]
        odd = tuple(i for i in range(3) if key[i] == 1)
        part = consts[index] * value
        if len(odd) == 3:
            n[key] = part
            continue
        if len(odd) == 0:
            balance = density
            for i in range(3):
                if key[i] == 2:
                    balance = balance + square[i]
        elif len(odd) == 1:
            balance = u[odd[0]]
        else:
            balance = product[odd]
        n[key] = part + consts[27 + index] * balance
    for axis in (0, 1, 2):
        n = along(n, axis, backward)
    return n, u


def turn(value, e):
    return value if e == 0 else pltpu.roll(value, 1 if e == 1 else LAST, 1)


def lane_of(e):
    return 0 if e == 1 else LAST


def both(lane, one, two):
    return jnp.where(lane == LAST, two, one)


def z_fields(place):
    if place < 9:
        return tuple(pop(place // 3, place % 3, e) for e in SIDES)
    return tuple(SOOT[2, e] + place - 9 for e in SIDES)


def layer_out(step, x, pops, soot_ref, growth, consts, F, center):
    rows = pl.ds(pl.multiple_of(16 * x + 24, 8), 8)
    g = {(k // 9, k // 3 % 3, k % 3): pops[k, x] for k in range(27)}
    n, u = collide(g, consts)
    for (a, b, e), value in n.items():
        F[step, pop(a, b, e), rows, :] = value
    half = [0.5 * v for v in u]
    for j in range(6):
        soot = soot_ref[j, x]
        for axis in range(3):
            F[step, SOOT[axis, 1] + j, rows, :] = soot * (KAPPA[j] + half[axis])
            F[step, SOOT[axis, 2] + j, rows, :] = soot * (KAPPA[j] - half[axis])
        center[j, x] = soot * (growth[x] + (1.0 - 6.0 * KAPPA[j]))


def turn_layer(step, x, F, zs):
    lane = lax.broadcasted_iota(jnp.int32, (8, 128), 1)
    rows = pl.ds(pl.multiple_of(16 * x + 24, 8), 8)
    past = lane - x
    packed = None
    for place in range(15):
        one, two = z_fields(place)
        plus, minus = F[step, one, rows, :], F[step, two, rows, :]
        F[step, one, rows, :] = turn(plus, 1)
        F[step, two, rows, :] = turn(minus, 2)
        moved = pltpu.roll(jnp.where(lane == 0, minus, plus), 8 * place + 1 + x, 1)
        packed = moved if place == 0 else jnp.where(past >= 8 * place, moved, packed)
    left = lax.rem(lane, 8)
    zs[step, 0] = jnp.where(left == x, packed, zs[step, 0])
    zs[step, 1] = jnp.where(left == lax.rem(x + 1, 8), packed, zs[step, 1])


def pull(step, x, F, center, pops, soot_ref):
    for a in range(3):
        for b in range(3):
            for e in range(3):
                pops[9 * a + 3 * b + e, x] = F[step, pop(a, b, e), pl.ds(16 * (x - SPEED[a]) + 24 - SPEED[b], 8), :]
    for j in range(6):
        total = center[j, x]
        for axis in range(3):
            for side in SIDES:
                move = (16, 1, 0)[axis] * SPEED[side]
                total = total + F[step, SOOT[axis, side] + j, pl.ds(16 * x + 24 - move, 8), :]
        soot_ref[j, x] = total


def kernel(
    pops_ref, soot_ref, growth_ref, rates_ref, pops, soot,
    R, F, C, xs, xzs, xzh, xys, xyh, xyzh, ys, yh, yzs, yzh, zs, zh, rates, consts, load_sem, send_sem, recv_sem,
):
    position = tuple(lax.axis_index(axis) for axis in ("gx", "gy", "gz"))
    counts = tuple(lax.axis_size(axis) for axis in ("gx", "gy", "gz"))

    def device(*move):
        return tuple(lax.rem(p + (m + n), n) for p, m, n in zip(position, move, counts))

    targets = [(i, j, k) for i in (0, 1, -1) for j in (0, 1, -1) for k in (0, 1) if (i, j, k) != (0, 0, 0)]
    barrier = pltpu.get_barrier_semaphore()
    for target in sorted(targets, key=lambda t: -abs(t[0])):
        pl.semaphore_signal(barrier, inc=1, device_id=device(*target), device_id_type=MESH)

    loads = [
        pltpu.make_async_copy(source, target, load_sem.at[i])
        for i, (source, target) in enumerate([(rates_ref, rates), (pops_ref, pops), (soot_ref, soot), (growth_ref, R)])
    ]
    for load in loads:
        load.start()
    zs[...] = jnp.zeros_like(zs)
    xys[...] = jnp.zeros_like(xys)

    lane = lax.broadcasted_iota(jnp.int32, (8, 128), 1)
    sublane = lax.broadcasted_iota(jnp.int32, (8, 128), 0)

    def message(step, index, source, target, move):
        return pltpu.make_async_remote_copy(
            src_ref=source,
            dst_ref=target,
            send_sem=send_sem.at[step, index],
            recv_sem=recv_sem.at[step, index],
            device_id=device(*move),
            device_id_type=MESH,
        )

    def messages_x(step):
        out = []
        for d, (a, b) in enumerate(CORNERS):
            out.append(message(step, XY + d, xys.at[step, d], xyh.at[step, d], (SPEED[a], SPEED[b], 0)))
        for a in SIDES:
            first, slot = (9, 0) if a == 1 else (24, 9)
            there = F.at[step, pl.ds(first, 15), pl.ds(block(slot), 8)]
            out.append(message(step, X + a - 1, xs.at[step, a - 1], there, (SPEED[a], 0, 0)))
        for d, (a, b) in enumerate(CORNERS):
            out.append(message(step, XYZ + d, xys.at[step, d], xyzh.at[step, d], (SPEED[a], SPEED[b], 1)))
        for a in SIDES:
            out.append(message(step, XZ + a - 1, xzs.at[step, a - 1], xzh.at[step, a - 1], (SPEED[a], 0, 1)))
        return out

    def messages_yz(step):
        out = []
        for b in SIDES:
            out.append(message(step, Y + b - 1, ys.at[step, b - 1], yh.at[step, b - 1], (0, SPEED[b], 0)))
        for b in SIDES:
            out.append(message(step, YZ + b - 1, yzs.at[step, b - 1], yzh.at[step, b - 1], (0, SPEED[b], 1)))
        out.append(message(step, Z, zs.at[step], zh.at[step], (0, 0, 1)))
        return out

    def packed_of(pairs):
        total = None
        for i, (one, two) in enumerate(pairs):
            value = both(lane, one, two)
            moved = pltpu.roll(value, 2 * i, 1) if i else value
            here = (lane == 2 * i) | (lane == (2 * i - 1) % 128)
            total = moved if total is None else jnp.where(here, moved, total)
        return total

    def unpacked(total, i):
        return pltpu.roll(total, 128 - 2 * i, 1) if i else total

    def pack_x(step):
        for a in SIDES:
            first, rows = (9, slice(block(8), block(8) + 8)) if a == 1 else (24, slice(block(1), block(1) + 8))
            values = [F[step, first + i, rows, :] for i in range(15)]
            for i in range(15):
                xs[step, a - 1, i] = values[i]
            xzs[step, a - 1] = packed_of([(values[3 * b + 1], values[3 * b + 2]) for b in range(3)])
        for d, (a, b) in enumerate(CORNERS):
            row = block(8 if a == 1 else 1) + (7 if b == 1 else 0)
            for e in range(3):
                xys[step, d, e : e + 1, :] = F[step, pop(a, b, e), row : row + 1, :]

    def pack_y(step):
        for b in SIDES:
            row = block(1) + (7 if b == 1 else 0)
            pairs = []
            for a in range(3):
                found = [F[step, pop(a, b, e), pl.ds(row, 8, stride=16), :] for e in range(3)]
                for e in range(3):
                    ys[step, b - 1, 3 * a + e] = found[e]
                pairs.append((found[1], found[2]))
            yzs[step, b - 1] = packed_of(pairs)
            for j in range(6):
                ys[step, b - 1, 9 + j] = F[step, SOOT[1, b] + j, pl.ds(row, 8, stride=16), :]

    def fix_yz(step):
        for copy in messages_yz(step):
            copy.wait_recv()

        plus, minus = zh[step, 0], pltpu.roll(zh[step, 1], 126, 1)

        def fix_layers(i, carry):
            for x in (2 * i, 2 * i + 1):
                rows = pl.ds(pl.multiple_of(16 * x + 24, 8), 8)
                packed = jnp.where(lax.rem(lane, 8) == x, plus, minus)
                for place in range(15):
                    moved = pltpu.roll(packed, lax.rem(128 - 8 * place - x, 128), 1)
                    for e, field in zip(SIDES, z_fields(place)):
                        pltpu.store(F.at[step, field, rows, :], moved, mask=lane == lane_of(e))
            return carry

        lax.fori_loop(0, 4, fix_layers, 0)
        for b in SIDES:
            row = block(1) + (-1 if b == 1 else 8)
            packed = yzh[step, b - 1]
            for a in range(3):
                moved = unpacked(packed, a)
                for e in range(3):
                    value = yh[step, b - 1, 3 * a + e]
                    if e:
                        value = jnp.where(lane == lane_of(e), moved, value)
                    F[step, pop(a, b, e), pl.ds(row, 8, stride=16), :] = value
            for j in range(6):
                F[step, SOOT[1, b] + j, pl.ds(row, 8, stride=16), :] = yh[step, b - 1, 9 + j]

    def fix_x(step):
        for copy in messages_x(step):
            copy.wait_recv()
        for a in SIDES:
            slot = 0 if a == 1 else 9
            packed = xzh[step, a - 1]
            for b in range(3):
                moved = unpacked(packed, b)
                for e in SIDES:
                    there = F.at[step, pop(a, b, e), block(slot) : block(slot) + 8, :]
                    pltpu.store(there, moved, mask=lane == lane_of(e))
        other = ((sublane == 1) & (lane == 0)) | ((sublane == 2) & (lane == LAST))
        for d, (a, b) in enumerate(CORNERS):
            row = block(0 if a == 1 else 9) + (-1 if b == 1 else 8)
            value = jnp.where(other, xyzh[step, d], xyh[step, d])
            for e in range(3):
                F[step, pop(a, b, e), row : row + 1, :] = value[e : e + 1, :]

    for load in loads:
        load.wait()
    moment_constants(rates, consts)

    def one_pass(step, carry):
        @pl.when(step > 0)
        def _():
            fix_yz(step - 1)
            fix_x(step - 1)

        def two_layers(i, carry):
            layers = (jnp.where(i == 0, 0, 2 * i - 1), jnp.where(i == 0, 7, 2 * i))

            @pl.when(step > 0)
            def _():
                for x in layers:
                    pull(step - 1, x, F, C, pops, soot)

            @pl.when(step < STEPS)
            def _():
                for x in layers:
                    layer_out(step, x, pops, soot, R, consts, F, C)
                for x in layers:
                    turn_layer(step, x, F, zs)

            @pl.when((step < STEPS) & (i == 0))
            def _():
                pack_x(step)

                @pl.when(step == 0)
                def _():
                    pl.semaphore_wait(barrier, len(targets))

                for copy in messages_x(step):
                    copy.start()

            return carry

        lax.fori_loop(0, 4, two_layers, 0)

        @pl.when(step < STEPS)
        def _():
            pack_y(step)
            for copy in messages_yz(step):
                copy.start()

        return carry

    lax.fori_loop(0, STEPS + 1, one_pass, 0)

    def finish(step, carry):
        for copy in messages_x(step) + messages_yz(step):
            copy.wait_send()
        return carry

    lax.fori_loop(0, STEPS, finish, 0)


def write_back(pops_ref, soot_ref, pops_out, soot_out, sem):
    copies = [
        pltpu.make_async_copy(pops_ref, pops_out, sem.at[0]),
        pltpu.make_async_copy(soot_ref, soot_out, sem.at[1]),
    ]
    for copy in copies:
        copy.start()
    for copy in copies:
        copy.wait()


def shards(populations, soot_moments, growth_rate, moment_rates):
    f32 = jnp.float32
    hbm = pl.BlockSpec(memory_space=pl.ANY)
    vmem = pl.BlockSpec(memory_space=pltpu.VMEM)
    held = pl.pallas_call(
        kernel,
        out_shape=(pltpu.VMEM(populations.shape, f32), pltpu.VMEM(soot_moments.shape, f32)),
        in_specs=[hbm, hbm, hbm, hbm],
        out_specs=(vmem, vmem),
        scratch_shapes=[
            pltpu.VMEM(growth_rate.shape, f32),
            pltpu.VMEM((STEPS, FIELDS, ROWS, 128), f32),
            pltpu.VMEM(soot_moments.shape, f32),
            pltpu.VMEM((STEPS, 2, 15, 8, 128), f32),
            pltpu.VMEM((STEPS, 2, 8, 128), f32),
            pltpu.VMEM((STEPS, 2, 8, 128), f32),
            pltpu.VMEM((STEPS, 4, 8, 128), f32),
            pltpu.VMEM((STEPS, 4, 8, 128), f32),
            pltpu.VMEM((STEPS, 4, 8, 128), f32),
            pltpu.VMEM((STEPS, 2, 15, 8, 128), f32),
            pltpu.VMEM((STEPS, 2, 15, 8, 128), f32),
            pltpu.VMEM((STEPS, 2, 8, 128), f32),
            pltpu.VMEM((STEPS, 2, 8, 128), f32),
            pltpu.VMEM((STEPS, 2, 8, 128), f32),
            pltpu.VMEM((STEPS, 2, 8, 128), f32),
            pltpu.SMEM((27,), f32),
            pltpu.SMEM((54,), f32),
            pltpu.SemaphoreType.DMA((4,)),
            pltpu.SemaphoreType.DMA((STEPS, MESSAGES)),
            pltpu.SemaphoreType.DMA((STEPS, MESSAGES)),
        ],
        compiler_params=pltpu.CompilerParams(
            collective_id=0, has_side_effects=True
        ),
    )(populations, soot_moments, growth_rate, moment_rates)
    anywhere = pl.BlockSpec(memory_space=pl.ANY)
    return pl.pallas_call(
        write_back,
        out_shape=tuple(jax.ShapeDtypeStruct(a.shape, f32) for a in held),
        in_specs=[anywhere] * 2,
        out_specs=(pl.BlockSpec(memory_space=pltpu.HBM),) * 2,
        scratch_shapes=[pltpu.SemaphoreType.DMA((2,))],
        compiler_params=pltpu.CompilerParams(vmem_limit_bytes=1024 * 1024),
    )(*held)


def solution(mesh):
    in_specs = (P(None, "gx", "gy", "gz"), P(None, "gx", "gy", "gz"), P("gx", "gy", "gz"), P())
    out_specs = (P(None, "gx", "gy", "gz"), P(None, "gx", "gy", "gz"))
    return jax.shard_map(shards, mesh=mesh, in_specs=in_specs, out_specs=out_specs, check_vma=False)
```

```python
import functools

import jax
import jax.numpy as jnp
from jax import lax
from jax.experimental import pallas as pl
from jax.experimental.pallas import tpu as pltpu
from jax.sharding import PartitionSpec as P

MESH = pl.DeviceIdType.MESH
STEPS = 2
KAPPA = (0.08, 0.06, 0.05, 0.04, 0.035, 0.03)
SPEED = (0, 1, -1)
LAST = 127
SIDES = (1, 2)
CORNERS = ((1, 1), (1, 2), (2, 1), (2, 2))
SOOT = {(0, 1): 18, (0, 2): 33, (1, 1): 39, (1, 2): 45, (2, 1): 51, (2, 2): 57}
FIELDS = 63
ROWS = 168
X, XZ, XY, XYZ, Y, YZ, Z = 0, 2, 4, 8, 12, 14, 16
MESSAGES = 17


def pop(a, b, e):
    return (0, 9, 24)[a] + 3 * b + e


def block(slot):
    return 16 * slot + 8


def forward(f):
    total = f[1] + f[2]
    return (4.0 * f[0] + total, f[1] - f[2], total)


def backward(n):
    return (0.5 * (n[0] - n[2]), n[1] + n[2], n[2] - n[1])


def along(values, axis, change):
    out = {}
    for i in range(3):
        for j in range(3):
            keys = [(i, j)[:axis] + (k,) + (i, j)[axis:] for k in range(3)]
            for key, value in zip(keys, change([values[key] for key in keys])):
                out[key] = value
    return out


def moment_constants(rates_ref, consts):
    for index in range(27):
        powers = (index // 9, index // 3 % 3, index % 3)
        rate = rates_ref[index]
        consts[index] = 0.125 - 0.125 * rate
        consts[27 + index] = rate * (27.0 / 3.0 ** powers.count(2))


def collide(g, consts):
    m = g
    for axis in (2, 1, 0):
        m = along(m, axis, forward)
    scale = 1.0 / 216.0
    density = m[0, 0, 0] * scale
    u = (m[1, 0, 0] * scale, m[0, 1, 0] * scale, m[0, 0, 1] * scale)
    square = [3.0 * v * v for v in u]
    product = {(0, 1): u[0] * u[1], (0, 2): u[0] * u[2], (1, 2): u[1] * u[2]}
    n = {}
    for key, value in m.items():
        index = 9 * key[0] + 3 * key[1] + key[2]
        odd = tuple(i for i in range(3) if key[i] == 1)
        part = consts[index] * value
        if len(odd) == 3:
            n[key] = part
            continue
        if len(odd) == 0:
            balance = density
            for i in range(3):
                if key[i] == 2:
                    balance = balance + square[i]
        elif len(odd) == 1:
            balance = u[odd[0]]
        else:
            balance = product[odd]
        n[key] = part + consts[27 + index] * balance
    for axis in (0, 1, 2):
        n = along(n, axis, backward)
    return n, u


def turn(value, e):
    return value if e == 0 else pltpu.roll(value, 1 if e == 1 else LAST, 1)


def lane_of(e):
    return 0 if e == 1 else LAST


def both(lane, one, two):
    return jnp.where(lane == LAST, two, one)


def z_fields(place):
    if place < 9:
        return tuple(pop(place // 3, place % 3, e) for e in SIDES)
    return tuple(SOOT[2, e] + place - 9 for e in SIDES)


def layer_out(step, x, pops, soot_ref, growth, consts, F, center):
    rows = pl.ds(pl.multiple_of(16 * x + 24, 8), 8)
    g = {(k // 9, k // 3 % 3, k % 3): pops[k, x] for k in range(27)}
    n, u = collide(g, consts)
    for (a, b, e), value in n.items():
        F[step, pop(a, b, e), rows, :] = value
    half = [0.5 * v for v in u]
    for j in range(6):
        soot = soot_ref[j, x]
        for axis in range(3):
            F[step, SOOT[axis, 1] + j, rows, :] = soot * (KAPPA[j] + half[axis])
            F[step, SOOT[axis, 2] + j, rows, :] = soot * (KAPPA[j] - half[axis])
        center[j, x] = soot * (growth[x] + (1.0 - 6.0 * KAPPA[j]))


def turn_layer(step, x, F, zs):
    lane = lax.broadcasted_iota(jnp.int32, (8, 128), 1)
    rows = pl.ds(pl.multiple_of(16 * x + 24, 8), 8)
    past = lane - x
    packed = None
    for place in range(15):
        one, two = z_fields(place)
        plus, minus = F[step, one, rows, :], F[step, two, rows, :]
        F[step, one, rows, :] = turn(plus, 1)
        F[step, two, rows, :] = turn(minus, 2)
        moved = pltpu.roll(jnp.where(lane == 0, minus, plus), 8 * place + 1 + x, 1)
        packed = moved if place == 0 else jnp.where(past >= 8 * place, moved, packed)
    left = lax.rem(lane, 8)
    zs[step, 0] = jnp.where(left == x, packed, zs[step, 0])
    zs[step, 1] = jnp.where(left == lax.rem(x + 1, 8), packed, zs[step, 1])


def pull(step, x, F, center, pops, soot_ref):
    for a in range(3):
        for b in range(3):
            for e in range(3):
                pops[9 * a + 3 * b + e, x] = F[step, pop(a, b, e), pl.ds(16 * (x - SPEED[a]) + 24 - SPEED[b], 8), :]
    for j in range(6):
        total = center[j, x]
        for axis in range(3):
            for side in SIDES:
                move = (16, 1, 0)[axis] * SPEED[side]
                total = total + F[step, SOOT[axis, side] + j, pl.ds(16 * x + 24 - move, 8), :]
        soot_ref[j, x] = total


def kernel(
    pops_ref, soot_ref, growth_ref, rates_ref, pops, soot,
    R, F, C, xs, xzs, xzh, xys, xyh, xyzh, ys, yh, yzs, yzh, zs, zh, rates, consts, load_sem, send_sem, recv_sem,
):
    position = tuple(lax.axis_index(axis) for axis in ("gx", "gy", "gz"))
    counts = tuple(lax.axis_size(axis) for axis in ("gx", "gy", "gz"))

    def device(*move):
        return tuple(lax.rem(p + (m + n), n) for p, m, n in zip(position, move, counts))

    targets = [(i, j, k) for i in (0, 1, -1) for j in (0, 1, -1) for k in (0, 1) if (i, j, k) != (0, 0, 0)]
    barrier = pltpu.get_barrier_semaphore()
    for target in sorted(targets, key=lambda t: -abs(t[0])):
        pl.semaphore_signal(barrier, inc=1, device_id=device(*target), device_id_type=MESH)

    loads = [
        pltpu.make_async_copy(source, target, load_sem.at[i])
        for i, (source, target) in enumerate([(rates_ref, rates), (pops_ref, pops), (soot_ref, soot), (growth_ref, R)])
    ]
    for load in loads:
        load.start()
    zs[...] = jnp.zeros_like(zs)
    xys[...] = jnp.zeros_like(xys)

    lane = lax.broadcasted_iota(jnp.int32, (8, 128), 1)
    sublane = lax.broadcasted_iota(jnp.int32, (8, 128), 0)

    def message(step, index, source, target, move):
        return pltpu.make_async_remote_copy(
            src_ref=source,
            dst_ref=target,
            send_sem=send_sem.at[step, index],
            recv_sem=recv_sem.at[step, index],
            device_id=device(*move),
            device_id_type=MESH,
        )

    def messages_xy(step):
        out = []
        for d, (a, b) in enumerate(CORNERS):
            out.append(message(step, XY + d, xys.at[step, d], xyh.at[step, d], (SPEED[a], SPEED[b], 0)))
        for d, (a, b) in enumerate(CORNERS):
            out.append(message(step, XYZ + d, xys.at[step, d], xyzh.at[step, d], (SPEED[a], SPEED[b], 1)))
        return out

    def messages_x(step):
        out = []
        for a in SIDES:
            first, slot = (9, 0) if a == 1 else (24, 9)
            there = F.at[step, pl.ds(first, 15), pl.ds(block(slot), 8)]
            out.append(message(step, X + a - 1, xs.at[step, a - 1], there, (SPEED[a], 0, 0)))
        for a in SIDES:
            out.append(message(step, XZ + a - 1, xzs.at[step, a - 1], xzh.at[step, a - 1], (SPEED[a], 0, 1)))
        return out

    def messages_y(step):
        out = []
        for b in SIDES:
            out.append(message(step, Y + b - 1, ys.at[step, b - 1], yh.at[step, b - 1], (0, SPEED[b], 0)))
        for b in SIDES:
            out.append(message(step, YZ + b - 1, yzs.at[step, b - 1], yzh.at[step, b - 1], (0, SPEED[b], 1)))
        return out

    def message_z(step):
        return message(step, Z, zs.at[step], zh.at[step], (0, 0, 1))

    def send_x(step):
        for a in SIDES:
            first, rows = (9, slice(block(8), block(8) + 8)) if a == 1 else (24, slice(block(1), block(1) + 8))
            packed = None
            for b in range(3):
                raw = [F[step, pop(a, b, e), rows, :] for e in range(3)]
                moved = pltpu.roll(jnp.where(lane == 0, raw[2], raw[1]), 2 * b + 1, 1)
                packed = moved if b == 0 else jnp.where(lane >= 2 * b, moved, packed)
                for e in range(3):
                    xs[step, a - 1, 3 * b + e] = turn(raw[e], e)
            xzs[step, a - 1] = packed
            for i in range(9, 15):
                xs[step, a - 1, i] = F[step, first + i, rows, :]
        for d, (a, b) in enumerate(CORNERS):
            row = 7 if b == 1 else 0
            for e in range(3):
                xys[step, d, e : e + 1, :] = xs[step, a - 1, 3 * b + e, row : row + 1, :]

        @pl.when(step == 0)
        def _():
            pl.semaphore_wait(barrier, len(targets))

        far, near = messages_xy(step), messages_x(step)
        for copy in far + near[2:] + near[:2]:
            copy.start()

    def send_y(step):
        for b in SIDES:
            row = block(1) + (7 if b == 1 else 0)
            packed = None
            for a in range(3):
                raw = [F[step, pop(a, b, e), pl.ds(row, 8, stride=16), :] for e in range(3)]
                moved = pltpu.roll(jnp.where(lane == 0, raw[2], raw[1]), 2 * a + 1, 1)
                packed = moved if a == 0 else jnp.where(lane >= 2 * a, moved, packed)
                for e in range(3):
                    ys[step, b - 1, 3 * a + e] = turn(raw[e], e)
            yzs[step, b - 1] = packed
            for j in range(6):
                ys[step, b - 1, 9 + j] = F[step, SOOT[1, b] + j, pl.ds(row, 8, stride=16), :]
        for copy in messages_y(step):
            copy.start()

    def fix_z(step):
        message_z(step).wait_recv()
        plus, minus = zh[step, 0], pltpu.roll(zh[step, 1], 126, 1)

        def fix_layers(i, carry):
            for x in (2 * i, 2 * i + 1):
                rows = pl.ds(pl.multiple_of(16 * x + 24, 8), 8)
                packed = jnp.where(lax.rem(lane, 8) == x, plus, minus)
                for place in range(15):
                    moved = pltpu.roll(packed, lax.rem(128 - 8 * place - x, 128), 1)
                    for e, field in zip(SIDES, z_fields(place)):
                        pltpu.store(F.at[step, field, rows, :], moved, mask=lane == lane_of(e))
            return carry

        lax.fori_loop(0, 4, fix_layers, 0)

    def unpacked(packed, i, e):
        shift = (128 - 2 * i - (0 if e == 1 else 2)) % 128
        return pltpu.roll(packed, shift, 1) if shift else packed

    def fix_y(step):
        for copy in messages_y(step):
            copy.wait_recv()
        for b in SIDES:
            row = block(1) + (-1 if b == 1 else 8)
            for a in range(3):
                for e in range(3):
                    value = yh[step, b - 1, 3 * a + e]
                    if e:
                        value = jnp.where(lane == lane_of(e), unpacked(yzh[step, b - 1], a, e), value)
                    F[step, pop(a, b, e), pl.ds(row, 8, stride=16), :] = value
            for j in range(6):
                F[step, SOOT[1, b] + j, pl.ds(row, 8, stride=16), :] = yh[step, b - 1, 9 + j]

    def fix_x(step):
        for copy in messages_x(step):
            copy.wait_recv()
        for a in SIDES:
            slot = 0 if a == 1 else 9
            packed = xzh[step, a - 1]
            for b in range(3):
                for e in SIDES:
                    moved = unpacked(packed, b, e)
                    there = F.at[step, pop(a, b, e), block(slot) : block(slot) + 8, :]
                    pltpu.store(there, moved, mask=lane == lane_of(e))
        for copy in messages_xy(step):
            copy.wait_recv()
        other = ((sublane == 1) & (lane == 0)) | ((sublane == 2) & (lane == LAST))
        for d, (a, b) in enumerate(CORNERS):
            row = block(0 if a == 1 else 9) + (-1 if b == 1 else 8)
            value = jnp.where(other, xyzh[step, d], xyh[step, d])
            for e in range(3):
                F[step, pop(a, b, e), row : row + 1, :] = value[e : e + 1, :]

    for load in loads:
        load.wait()
    moment_constants(rates, consts)

    def one_pass(step, carry):
        @pl.when(step > 0)
        def _():
            fix_z(step - 1)
            fix_y(step - 1)

        @pl.when(step == STEPS)
        def _():
            for copy in messages_y(STEPS - 1) + [message_z(STEPS - 1)]:
                copy.wait_send()

        def two_layers(i, carry):
            i = lax.rem(i + jnp.where(step == STEPS, 1, 0), 4)
            layers = (jnp.where(i == 0, 0, 2 * i - 1), jnp.where(i == 0, 7, 2 * i))

            @pl.when((step > 0) & (i == 0))
            def _():
                fix_x(step - 1)

            @pl.when(step > 0)
            def _():
                for x in layers:
                    pull(step - 1, x, F, C, pops, soot)

            @pl.when(step < STEPS)
            def _():
                for x in layers:
                    layer_out(step, x, pops, soot, R, consts, F, C)

            @pl.when((step < STEPS) & (i == 0))
            def _():
                send_x(step)

            return carry

        lax.fori_loop(0, 4, two_layers, 0)

        @pl.when(step < STEPS)
        def _():
            send_y(step)

            def turn_layers(i, carry):
                for x in (2 * i, 2 * i + 1):
                    turn_layer(step, x, F, zs)
                return carry

            lax.fori_loop(0, 4, turn_layers, 0)
            message_z(step).start()

        @pl.when((step > 0) & (step < STEPS))
        def _():
            for copy in messages_xy(step - 1) + messages_x(step - 1) + messages_y(step - 1) + [message_z(step - 1)]:
                copy.wait_send()

        return carry

    lax.fori_loop(0, STEPS + 1, one_pass, 0)
    for copy in messages_xy(STEPS - 1) + messages_x(STEPS - 1):
        copy.wait_send()


def write_back(pops_ref, soot_ref, pops_out, soot_out, sem):
    copies = [
        pltpu.make_async_copy(pops_ref, pops_out, sem.at[0]),
        pltpu.make_async_copy(soot_ref, soot_out, sem.at[1]),
    ]
    for copy in copies:
        copy.start()
    for copy in copies:
        copy.wait()


def shards(populations, soot_moments, growth_rate, moment_rates):
    f32 = jnp.float32
    hbm = pl.BlockSpec(memory_space=pl.ANY)
    vmem = pl.BlockSpec(memory_space=pltpu.VMEM)
    held = pl.pallas_call(
        kernel,
        out_shape=(pltpu.VMEM(populations.shape, f32), pltpu.VMEM(soot_moments.shape, f32)),
        in_specs=[hbm, hbm, hbm, hbm],
        out_specs=(vmem, vmem),
        scratch_shapes=[
            pltpu.VMEM(growth_rate.shape, f32),
            pltpu.VMEM((STEPS, FIELDS, ROWS, 128), f32),
            pltpu.VMEM(soot_moments.shape, f32),
            pltpu.VMEM((STEPS, 2, 15, 8, 128), f32),
            pltpu.VMEM((STEPS, 2, 8, 128), f32),
            pltpu.VMEM((STEPS, 2, 8, 128), f32),
            pltpu.VMEM((STEPS, 4, 8, 128), f32),
            pltpu.VMEM((STEPS, 4, 8, 128), f32),
            pltpu.VMEM((STEPS, 4, 8, 128), f32),
            pltpu.VMEM((STEPS, 2, 15, 8, 128), f32),
            pltpu.VMEM((STEPS, 2, 15, 8, 128), f32),
            pltpu.VMEM((STEPS, 2, 8, 128), f32),
            pltpu.VMEM((STEPS, 2, 8, 128), f32),
            pltpu.VMEM((STEPS, 2, 8, 128), f32),
            pltpu.VMEM((STEPS, 2, 8, 128), f32),
            pltpu.SMEM((27,), f32),
            pltpu.SMEM((54,), f32),
            pltpu.SemaphoreType.DMA((4,)),
            pltpu.SemaphoreType.DMA((STEPS, MESSAGES)),
            pltpu.SemaphoreType.DMA((STEPS, MESSAGES)),
        ],
        compiler_params=pltpu.CompilerParams(
            collective_id=0, has_side_effects=True
        ),
    )(populations, soot_moments, growth_rate, moment_rates)
    anywhere = pl.BlockSpec(memory_space=pl.ANY)
    return pl.pallas_call(
        write_back,
        out_shape=tuple(jax.ShapeDtypeStruct(a.shape, f32) for a in held),
        in_specs=[anywhere] * 2,
        out_specs=(pl.BlockSpec(memory_space=pltpu.HBM),) * 2,
        scratch_shapes=[pltpu.SemaphoreType.DMA((2,))],
        compiler_params=pltpu.CompilerParams(vmem_limit_bytes=1024 * 1024),
    )(*held)


def solution(mesh):
    in_specs = (P(None, "gx", "gy", "gz"), P(None, "gx", "gy", "gz"), P("gx", "gy", "gz"), P())
    out_specs = (P(None, "gx", "gy", "gz"), P(None, "gx", "gy", "gz"))
    return jax.shard_map(shards, mesh=mesh, in_specs=in_specs, out_specs=out_specs, check_vma=False)
```

```python
import functools

import jax
import jax.numpy as jnp
from jax import lax
from jax.experimental import pallas as pl
from jax.experimental.pallas import tpu as pltpu
from jax.sharding import PartitionSpec as P

MESH = pl.DeviceIdType.MESH
STEPS = 2
KAPPA = (0.08, 0.06, 0.05, 0.04, 0.035, 0.03)
SPEED = (0, 1, -1)
LAST = 127
SIDES = (1, 2)
CORNERS = ((1, 1), (1, 2), (2, 1), (2, 2))
SOOT = {(0, 1): 18, (0, 2): 33, (1, 1): 39, (1, 2): 45, (2, 1): 51, (2, 2): 57}
FIELDS = 63
ROWS = 168
X, XZ, XY, XYZ, Y, YZ, Z = 0, 2, 4, 8, 12, 14, 16
MESSAGES = 17


def pop(a, b, e):
    return (0, 9, 24)[a] + 3 * b + e


def block(slot):
    return 16 * slot + 8


def forward(f):
    total = f[1] + f[2]
    return (4.0 * f[0] + total, f[1] - f[2], total)


def backward(n):
    return (0.5 * (n[0] - n[2]), n[1] + n[2], n[2] - n[1])


def along(values, axis, change):
    out = {}
    for i in range(3):
        for j in range(3):
            keys = [(i, j)[:axis] + (k,) + (i, j)[axis:] for k in range(3)]
            for key, value in zip(keys, change([values[key] for key in keys])):
                out[key] = value
    return out


def moment_constants(rates_ref, consts):
    for index in range(27):
        powers = (index // 9, index // 3 % 3, index % 3)
        rate = rates_ref[index]
        consts[index] = 0.125 - 0.125 * rate
        consts[27 + index] = rate * (27.0 / 3.0 ** powers.count(2))


def collide(g, consts):
    m = g
    for axis in (2, 1, 0):
        m = along(m, axis, forward)
    scale = 1.0 / 216.0
    density = m[0, 0, 0] * scale
    u = (m[1, 0, 0] * scale, m[0, 1, 0] * scale, m[0, 0, 1] * scale)
    square = [3.0 * v * v for v in u]
    product = {(0, 1): u[0] * u[1], (0, 2): u[0] * u[2], (1, 2): u[1] * u[2]}
    n = {}
    for key, value in m.items():
        index = 9 * key[0] + 3 * key[1] + key[2]
        odd = tuple(i for i in range(3) if key[i] == 1)
        part = consts[index] * value
        if len(odd) == 3:
            n[key] = part
            continue
        if len(odd) == 0:
            balance = density
            for i in range(3):
                if key[i] == 2:
                    balance = balance + square[i]
        elif len(odd) == 1:
            balance = u[odd[0]]
        else:
            balance = product[odd]
        n[key] = part + consts[27 + index] * balance
    for axis in (0, 1, 2):
        n = along(n, axis, backward)
    return n, u


def turn(value, e):
    return value if e == 0 else pltpu.roll(value, 1 if e == 1 else LAST, 1)


def lane_of(e):
    return 0 if e == 1 else LAST


def both(lane, one, two):
    return jnp.where(lane == LAST, two, one)


def z_fields(place):
    if place < 9:
        return tuple(pop(place // 3, place % 3, e) for e in SIDES)
    return tuple(SOOT[2, e] + place - 9 for e in SIDES)


def layer_out(step, x, pops, soot_ref, growth, consts, F, center):
    rows = pl.ds(pl.multiple_of(16 * x + 24, 8), 8)
    g = {(k // 9, k // 3 % 3, k % 3): pops[k, x] for k in range(27)}
    n, u = collide(g, consts)
    for (a, b, e), value in n.items():
        F[step, pop(a, b, e), rows, :] = value
    half = [0.5 * v for v in u]
    for j in range(6):
        soot = soot_ref[j, x]
        for axis in range(3):
            F[step, SOOT[axis, 1] + j, rows, :] = soot * (KAPPA[j] + half[axis])
            F[step, SOOT[axis, 2] + j, rows, :] = soot * (KAPPA[j] - half[axis])
        center[j, x] = soot * (growth[x] + (1.0 - 6.0 * KAPPA[j]))


def turn_layer(step, x, F, zs):
    lane = lax.broadcasted_iota(jnp.int32, (8, 128), 1)
    rows = pl.ds(pl.multiple_of(16 * x + 24, 8), 8)
    past = lane - x
    packed = None
    for place in range(15):
        one, two = z_fields(place)
        plus, minus = F[step, one, rows, :], F[step, two, rows, :]
        F[step, one, rows, :] = turn(plus, 1)
        F[step, two, rows, :] = turn(minus, 2)
        moved = pltpu.roll(jnp.where(lane == 0, minus, plus), 8 * place + 1 + x, 1)
        packed = moved if place == 0 else jnp.where(past >= 8 * place, moved, packed)
    left = lane & 7
    zs[step, 0] = jnp.where(left == x, packed, zs[step, 0])
    zs[step, 1] = jnp.where(left == ((x + 1) & 7), packed, zs[step, 1])


def pull(step, x, F, center, pops, soot_ref):
    for a in range(3):
        for b in range(3):
            for e in range(3):
                pops[9 * a + 3 * b + e, x] = F[step, pop(a, b, e), pl.ds(16 * (x - SPEED[a]) + 24 - SPEED[b], 8), :]
    for j in range(6):
        total = center[j, x]
        for axis in range(3):
            for side in SIDES:
                move = (16, 1, 0)[axis] * SPEED[side]
                total = total + F[step, SOOT[axis, side] + j, pl.ds(16 * x + 24 - move, 8), :]
        soot_ref[j, x] = total


def kernel(
    pops_ref, soot_ref, growth_ref, rates_ref, pops, soot,
    R, F, C, xs, xzs, xzh, xys, xyh, xyzh, ys, yh, yzs, yzh, zs, zh, rates, consts, load_sem, send_sem, recv_sem,
):
    position = tuple(lax.axis_index(axis) for axis in ("gx", "gy", "gz"))
    counts = tuple(lax.axis_size(axis) for axis in ("gx", "gy", "gz"))

    near = [{0: p, 1: lax.rem(p + 1, n), -1: lax.rem(p + (n - 1), n)} for p, n in zip(position, counts)]

    def device(*move):
        return tuple(at[m] for at, m in zip(near, move))

    targets = [(i, j, k) for i in (0, 1, -1) for j in (0, 1, -1) for k in (0, 1) if (i, j, k) != (0, 0, 0)]
    barrier = pltpu.get_barrier_semaphore()
    for target in sorted(targets, key=lambda t: -abs(t[0])):
        pl.semaphore_signal(barrier, inc=1, device_id=device(*target), device_id_type=MESH)

    loads = [
        pltpu.make_async_copy(source, target, load_sem.at[i])
        for i, (source, target) in enumerate([(rates_ref, rates), (pops_ref, pops), (soot_ref, soot), (growth_ref, R)])
    ]
    for load in loads:
        load.start()
    zs[...] = jnp.zeros_like(zs)
    xys[...] = jnp.zeros_like(xys)

    lane = lax.broadcasted_iota(jnp.int32, (8, 128), 1)
    sublane = lax.broadcasted_iota(jnp.int32, (8, 128), 0)

    def message(step, index, source, target, move):
        return pltpu.make_async_remote_copy(
            src_ref=source,
            dst_ref=target,
            send_sem=send_sem.at[step, index],
            recv_sem=recv_sem.at[step, index],
            device_id=device(*move),
            device_id_type=MESH,
        )

    def messages_xy(step):
        out = []
        for d, (a, b) in enumerate(CORNERS):
            out.append(message(step, XY + d, xys.at[step, d], xyh.at[step, d], (SPEED[a], SPEED[b], 0)))
        for d, (a, b) in enumerate(CORNERS):
            out.append(message(step, XYZ + d, xys.at[step, d], xyzh.at[step, d], (SPEED[a], SPEED[b], 1)))
        return out

    def messages_x(step):
        out = []
        for a in SIDES:
            first, slot = (9, 0) if a == 1 else (24, 9)
            there = F.at[step, pl.ds(first, 15), pl.ds(block(slot), 8)]
            out.append(message(step, X + a - 1, xs.at[step, a - 1], there, (SPEED[a], 0, 0)))
        for a in SIDES:
            out.append(message(step, XZ + a - 1, xzs.at[step, a - 1], xzh.at[step, a - 1], (SPEED[a], 0, 1)))
        return out

    def messages_y(step):
        out = []
        for b in SIDES:
            out.append(message(step, Y + b - 1, ys.at[step, b - 1], yh.at[step, b - 1], (0, SPEED[b], 0)))
        for b in SIDES:
            out.append(message(step, YZ + b - 1, yzs.at[step, b - 1], yzh.at[step, b - 1], (0, SPEED[b], 1)))
        return out

    def message_z(step):
        return message(step, Z, zs.at[step], zh.at[step], (0, 0, 1))

    def send_x(step):
        for d, (a, b) in enumerate(CORNERS):
            first = block(8 if a == 1 else 1)
            row = 7 if b == 1 else 0
            for e in range(3):
                value = turn(F[step, pop(a, b, e), first : first + 8, :], e)
                xys[step, d, e : e + 1, :] = value[row : row + 1, :]

        @pl.when(step == 0)
        def _():
            pl.semaphore_wait(barrier, len(targets))

        for copy in messages_xy(step):
            copy.start()
        for a in SIDES:
            first, rows = (9, slice(block(8), block(8) + 8)) if a == 1 else (24, slice(block(1), block(1) + 8))
            packed = None
            for b in range(3):
                raw = [F[step, pop(a, b, e), rows, :] for e in range(3)]
                moved = pltpu.roll(jnp.where(lane == 0, raw[2], raw[1]), 2 * b + 1, 1)
                packed = moved if b == 0 else jnp.where(lane >= 2 * b, moved, packed)
                for e in range(3):
                    xs[step, a - 1, 3 * b + e] = turn(raw[e], e)
            xzs[step, a - 1] = packed
            for i in range(9, 15):
                xs[step, a - 1, i] = F[step, first + i, rows, :]
        faces = messages_x(step)
        for copy in faces:
            copy.start()

    def send_y(step):
        for b in SIDES:
            row = block(1) + (7 if b == 1 else 0)
            packed = None
            for a in range(3):
                raw = [F[step, pop(a, b, e), pl.ds(row, 8, stride=16), :] for e in range(3)]
                moved = pltpu.roll(jnp.where(lane == 0, raw[2], raw[1]), 2 * a + 1, 1)
                packed = moved if a == 0 else jnp.where(lane >= 2 * a, moved, packed)
                for e in range(3):
                    ys[step, b - 1, 3 * a + e] = turn(raw[e], e)
            yzs[step, b - 1] = packed
            for j in range(6):
                ys[step, b - 1, 9 + j] = F[step, SOOT[1, b] + j, pl.ds(row, 8, stride=16), :]
        for copy in messages_y(step):
            copy.start()

    def fix_z(step):
        message_z(step).wait()
        plus, minus = zh[step, 0], pltpu.roll(zh[step, 1], 126, 1)

        def fix_layers(i, carry):
            for x in (2 * i, 2 * i + 1):
                rows = pl.ds(pl.multiple_of(16 * x + 24, 8), 8)
                packed = jnp.where(lane & 7 == x, plus, minus)
                for place in range(15):
                    moved = pltpu.roll(packed, (128 - 8 * place - x) & 127, 1)
                    for e, field in zip(SIDES, z_fields(place)):
                        pltpu.store(F.at[step, field, rows, :], moved, mask=lane == lane_of(e))
            return carry

        lax.fori_loop(0, 4, fix_layers, 0)

    def unpacked(packed, i, e):
        shift = (128 - 2 * i - (0 if e == 1 else 2)) % 128
        return pltpu.roll(packed, shift, 1) if shift else packed

    def fix_y(step):
        for copy in messages_y(step):
            copy.wait()
        for b in SIDES:
            row = block(1) + (-1 if b == 1 else 8)
            for a in range(3):
                for e in range(3):
                    value = yh[step, b - 1, 3 * a + e]
                    if e:
                        value = jnp.where(lane == lane_of(e), unpacked(yzh[step, b - 1], a, e), value)
                    F[step, pop(a, b, e), pl.ds(row, 8, stride=16), :] = value
            for j in range(6):
                F[step, SOOT[1, b] + j, pl.ds(row, 8, stride=16), :] = yh[step, b - 1, 9 + j]

    def fix_x(step):
        for copy in messages_x(step):
            copy.wait()
        for a in SIDES:
            slot = 0 if a == 1 else 9
            packed = xzh[step, a - 1]
            for b in range(3):
                for e in SIDES:
                    moved = unpacked(packed, b, e)
                    there = F.at[step, pop(a, b, e), block(slot) : block(slot) + 8, :]
                    pltpu.store(there, moved, mask=lane == lane_of(e))

    def fix_xy(step):
        far = messages_xy(step)
        for copy in far[4:] + far[:4]:
            copy.wait()
        other = ((sublane == 1) & (lane == 0)) | ((sublane == 2) & (lane == LAST))
        for d, (a, b) in enumerate(CORNERS):
            x, row = 0 if a == 1 else 7, 0 if b == 1 else 7
            value = jnp.where(other, xyzh[step, d], xyh[step, d])
            for e in range(3):
                pops[9 * a + 3 * b + e, x, row : row + 1, :] = value[e : e + 1, :]

    for load in loads:
        load.wait()
    moment_constants(rates, consts)

    def one_pass(step, carry):
        @pl.when(step > 0)
        def _():
            fix_z(step - 1)
            fix_y(step - 1)

        def two_layers(i, carry):
            i = lax.rem(i + jnp.where(step == STEPS, 1, 0), 4)
            layers = (jnp.where(i == 0, 0, 2 * i - 1), jnp.where(i == 0, 7, 2 * i))

            @pl.when((step > 0) & (i == 0))
            def _():
                fix_x(step - 1)

            @pl.when(step > 0)
            def _():
                for x in layers:
                    pull(step - 1, x, F, C, pops, soot)

            @pl.when((step > 0) & (i == 0))
            def _():
                fix_xy(step - 1)

            @pl.when(step < STEPS)
            def _():
                for x in layers:
                    layer_out(step, x, pops, soot, R, consts, F, C)

            @pl.when((step < STEPS) & (i == 0))
            def _():
                send_x(step)

            return carry

        lax.fori_loop(0, 4, two_layers, 0)

        @pl.when(step < STEPS)
        def _():
            send_y(step)

            def turn_layers(i, carry):
                for x in (2 * i, 2 * i + 1):
                    turn_layer(step, x, F, zs)
                return carry

            lax.fori_loop(0, 4, turn_layers, 0)
            message_z(step).start()

        return carry

    lax.fori_loop(0, STEPS + 1, one_pass, 0)


def write_back(pops_ref, soot_ref, pops_out, soot_out, sem):
    copies = [
        pltpu.make_async_copy(pops_ref, pops_out, sem.at[0]),
        pltpu.make_async_copy(soot_ref, soot_out, sem.at[1]),
    ]
    for copy in copies:
        copy.start()
    for copy in copies:
        copy.wait()


def shards(populations, soot_moments, growth_rate, moment_rates):
    f32 = jnp.float32
    hbm = pl.BlockSpec(memory_space=pl.ANY)
    vmem = pl.BlockSpec(memory_space=pltpu.VMEM)
    held = pl.pallas_call(
        kernel,
        out_shape=(pltpu.VMEM(populations.shape, f32), pltpu.VMEM(soot_moments.shape, f32)),
        in_specs=[hbm, hbm, hbm, hbm],
        out_specs=(vmem, vmem),
        scratch_shapes=[
            pltpu.VMEM(growth_rate.shape, f32),
            pltpu.VMEM((STEPS, FIELDS, ROWS, 128), f32),
            pltpu.VMEM(soot_moments.shape, f32),
            pltpu.VMEM((STEPS, 2, 15, 8, 128), f32),
            pltpu.VMEM((STEPS, 2, 8, 128), f32),
            pltpu.VMEM((STEPS, 2, 8, 128), f32),
            pltpu.VMEM((STEPS, 4, 8, 128), f32),
            pltpu.VMEM((STEPS, 4, 8, 128), f32),
            pltpu.VMEM((STEPS, 4, 8, 128), f32),
            pltpu.VMEM((STEPS, 2, 15, 8, 128), f32),
            pltpu.VMEM((STEPS, 2, 15, 8, 128), f32),
            pltpu.VMEM((STEPS, 2, 8, 128), f32),
            pltpu.VMEM((STEPS, 2, 8, 128), f32),
            pltpu.VMEM((STEPS, 2, 8, 128), f32),
            pltpu.VMEM((STEPS, 2, 8, 128), f32),
            pltpu.SMEM((27,), f32),
            pltpu.SMEM((54,), f32),
            pltpu.SemaphoreType.DMA((4,)),
            pltpu.SemaphoreType.DMA((STEPS, MESSAGES)),
            pltpu.SemaphoreType.DMA((STEPS, MESSAGES)),
        ],
        compiler_params=pltpu.CompilerParams(
            collective_id=0, has_side_effects=True
        ),
    )(populations, soot_moments, growth_rate, moment_rates)
    anywhere = pl.BlockSpec(memory_space=pl.ANY)
    return pl.pallas_call(
        write_back,
        out_shape=tuple(jax.ShapeDtypeStruct(a.shape, f32) for a in held),
        in_specs=[anywhere] * 2,
        out_specs=(pl.BlockSpec(memory_space=pltpu.HBM),) * 2,
        scratch_shapes=[pltpu.SemaphoreType.DMA((2,))],
        compiler_params=pltpu.CompilerParams(vmem_limit_bytes=1024 * 1024),
    )(*held)


def solution(mesh):
    in_specs = (P(None, "gx", "gy", "gz"), P(None, "gx", "gy", "gz"), P("gx", "gy", "gz"), P())
    out_specs = (P(None, "gx", "gy", "gz"), P(None, "gx", "gy", "gz"))
    return jax.shard_map(shards, mesh=mesh, in_specs=in_specs, out_specs=out_specs, check_vma=False)
```

```python
import functools

import jax
import jax.numpy as jnp
from jax import lax
from jax.experimental import pallas as pl
from jax.experimental.pallas import tpu as pltpu
from jax.sharding import PartitionSpec as P

MESH = pl.DeviceIdType.MESH
STEPS = 2
KAPPA = (0.08, 0.06, 0.05, 0.04, 0.035, 0.03)
SPEED = (0, 1, -1)
LAST = 127
SIDES = (1, 2)
CORNERS = ((1, 1), (1, 2), (2, 1), (2, 2))
SOOT = {(0, 1): 18, (0, 2): 33, (1, 1): 39, (1, 2): 45, (2, 1): 51, (2, 2): 57}
FIELDS = 63
ROWS = 168
X, XZ, XY, XYZ, Y, YZ, Z = 0, 2, 4, 8, 12, 14, 16
MESSAGES = 17


def pop(a, b, e):
    return (0, 9, 24)[a] + 3 * b + e


def block(slot):
    return 16 * slot + 8


def forward(f):
    total = f[1] + f[2]
    return (4.0 * f[0] + total, f[1] - f[2], total)


def backward(n):
    return (0.5 * (n[0] - n[2]), n[1] + n[2], n[2] - n[1])


def along(values, axis, change):
    out = {}
    for i in range(3):
        for j in range(3):
            keys = [(i, j)[:axis] + (k,) + (i, j)[axis:] for k in range(3)]
            for key, value in zip(keys, change([values[key] for key in keys])):
                out[key] = value
    return out


def moment_constants(rates_ref, consts):
    for index in range(27):
        powers = (index // 9, index // 3 % 3, index % 3)
        rate = rates_ref[index]
        consts[index] = 0.125 - 0.125 * rate
        consts[27 + index] = rate * (27.0 / 3.0 ** powers.count(2))


def collide(g, consts):
    m = g
    for axis in (2, 1, 0):
        m = along(m, axis, forward)
    scale = 1.0 / 216.0
    density = m[0, 0, 0] * scale
    u = (m[1, 0, 0] * scale, m[0, 1, 0] * scale, m[0, 0, 1] * scale)
    square = [3.0 * v * v for v in u]
    product = {(0, 1): u[0] * u[1], (0, 2): u[0] * u[2], (1, 2): u[1] * u[2]}
    n = {}
    for key, value in m.items():
        index = 9 * key[0] + 3 * key[1] + key[2]
        odd = tuple(i for i in range(3) if key[i] == 1)
        part = consts[index] * value
        if len(odd) == 3:
            n[key] = part
            continue
        if len(odd) == 0:
            balance = density
            for i in range(3):
                if key[i] == 2:
                    balance = balance + square[i]
        elif len(odd) == 1:
            balance = u[odd[0]]
        else:
            balance = product[odd]
        n[key] = part + consts[27 + index] * balance
    for axis in (0, 1, 2):
        n = along(n, axis, backward)
    return n, u


def turn(value, e):
    return value if e == 0 else pltpu.roll(value, 1 if e == 1 else LAST, 1)


def lane_of(e):
    return 0 if e == 1 else LAST


def both(lane, one, two):
    return jnp.where(lane == LAST, two, one)


def z_fields(place):
    if place < 9:
        return tuple(pop(place // 3, place % 3, e) for e in SIDES)
    return tuple(SOOT[2, e] + place - 9 for e in SIDES)


def layer_out(step, x, pops, consts, F, U):
    rows = pl.ds(pl.multiple_of(16 * x + 24, 8), 8)
    g = {(k // 9, k // 3 % 3, k % 3): pops[k, x] for k in range(27)}
    n, u = collide(g, consts)
    for (a, b, e), value in n.items():
        F[step, pop(a, b, e), rows, :] = value
    for axis in range(3):
        U[axis, x] = u[axis]


def soot_out(step, x, soot_ref, growth, F, center, U):
    rows = pl.ds(pl.multiple_of(16 * x + 24, 8), 8)
    half = [0.5 * U[axis, x] for axis in range(3)]
    for j in range(6):
        soot = soot_ref[j, x]
        for axis in range(3):
            F[step, SOOT[axis, 1] + j, rows, :] = soot * (KAPPA[j] + half[axis])
            F[step, SOOT[axis, 2] + j, rows, :] = soot * (KAPPA[j] - half[axis])
        center[j, x] = soot * (growth[x] + (1.0 - 6.0 * KAPPA[j]))


def turn_layer(step, x, F, zs):
    lane = lax.broadcasted_iota(jnp.int32, (8, 128), 1)
    rows = pl.ds(pl.multiple_of(16 * x + 24, 8), 8)
    past = lane - x
    packed = None
    for place in range(15):
        one, two = z_fields(place)
        plus, minus = F[step, one, rows, :], F[step, two, rows, :]
        F[step, one, rows, :] = turn(plus, 1)
        F[step, two, rows, :] = turn(minus, 2)
        moved = pltpu.roll(jnp.where(lane == 0, minus, plus), 8 * place + 1 + x, 1)
        packed = moved if place == 0 else jnp.where(past >= 8 * place, moved, packed)
    left = lane & 7
    zs[step, 0] = jnp.where(left == x, packed, zs[step, 0])
    zs[step, 1] = jnp.where(left == ((x + 1) & 7), packed, zs[step, 1])


def pull(step, x, F, center, pops, soot_ref):
    for a in range(3):
        for b in range(3):
            for e in range(3):
                pops[9 * a + 3 * b + e, x] = F[step, pop(a, b, e), pl.ds(16 * (x - SPEED[a]) + 24 - SPEED[b], 8), :]
    for j in range(6):
        total = center[j, x]
        for axis in range(3):
            for side in SIDES:
                move = (16, 1, 0)[axis] * SPEED[side]
                total = total + F[step, SOOT[axis, side] + j, pl.ds(16 * x + 24 - move, 8), :]
        soot_ref[j, x] = total


def kernel(
    pops_ref, soot_ref, growth_ref, rates_ref, pops, soot,
    R, F, C, U, xs, xzs, xzh, xys, xyh, xyzh, ys, yh, yzs, yzh, zs, zh, rates, consts, load_sem, send_sem, recv_sem,
):
    position = tuple(lax.axis_index(axis) for axis in ("gx", "gy", "gz"))
    counts = tuple(lax.axis_size(axis) for axis in ("gx", "gy", "gz"))

    near = [{0: p, 1: lax.rem(p + 1, n), -1: lax.rem(p + (n - 1), n)} for p, n in zip(position, counts)]

    def device(*move):
        return tuple(at[m] for at, m in zip(near, move))

    targets = [(i, j, k) for i in (0, 1, -1) for j in (0, 1, -1) for k in (0, 1) if (i, j, k) != (0, 0, 0)]
    barrier = pltpu.get_barrier_semaphore()
    for target in sorted(targets, key=lambda t: -abs(t[0])):
        pl.semaphore_signal(barrier, inc=1, device_id=device(*target), device_id_type=MESH)

    loads = [
        pltpu.make_async_copy(source, target, load_sem.at[i])
        for i, (source, target) in enumerate([(rates_ref, rates), (pops_ref, pops), (soot_ref, soot), (growth_ref, R)])
    ]
    for load in loads:
        load.start()
    zs[...] = jnp.zeros_like(zs)
    xys[...] = jnp.zeros_like(xys)

    lane = lax.broadcasted_iota(jnp.int32, (8, 128), 1)
    sublane = lax.broadcasted_iota(jnp.int32, (8, 128), 0)

    def message(step, index, source, target, move):
        return pltpu.make_async_remote_copy(
            src_ref=source,
            dst_ref=target,
            send_sem=send_sem.at[step, index],
            recv_sem=recv_sem.at[step, index],
            device_id=device(*move),
            device_id_type=MESH,
        )

    def messages_xy(step):
        out = []
        for d, (a, b) in enumerate(CORNERS):
            out.append(message(step, XY + d, xys.at[step, d], xyh.at[step, d], (SPEED[a], SPEED[b], 0)))
        for d, (a, b) in enumerate(CORNERS):
            out.append(message(step, XYZ + d, xys.at[step, d], xyzh.at[step, d], (SPEED[a], SPEED[b], 1)))
        return out

    def messages_x(step):
        out = []
        for a in SIDES:
            first, slot = (9, 0) if a == 1 else (24, 9)
            there = F.at[step, pl.ds(first, 15), pl.ds(block(slot), 8)]
            out.append(message(step, X + a - 1, xs.at[step, a - 1], there, (SPEED[a], 0, 0)))
        for a in SIDES:
            out.append(message(step, XZ + a - 1, xzs.at[step, a - 1], xzh.at[step, a - 1], (SPEED[a], 0, 1)))
        return out

    def messages_y(step):
        out = []
        for b in SIDES:
            out.append(message(step, Y + b - 1, ys.at[step, b - 1], yh.at[step, b - 1], (0, SPEED[b], 0)))
        for b in SIDES:
            out.append(message(step, YZ + b - 1, yzs.at[step, b - 1], yzh.at[step, b - 1], (0, SPEED[b], 1)))
        return out

    def message_z(step):
        return message(step, Z, zs.at[step], zh.at[step], (0, 0, 1))

    def send_edges(step):
        for d, (a, b) in enumerate(CORNERS):
            first = block(8 if a == 1 else 1)
            row = 7 if b == 1 else 0
            for e in range(3):
                value = turn(F[step, pop(a, b, e), first : first + 8, :], e)
                xys[step, d, e : e + 1, :] = value[row : row + 1, :]

        @pl.when(step == 0)
        def _():
            pl.semaphore_wait(barrier, len(targets))

        for copy in messages_xy(step):
            copy.start()

    def send_x(step):
        for a in SIDES:
            first, rows = (9, slice(block(8), block(8) + 8)) if a == 1 else (24, slice(block(1), block(1) + 8))
            packed = None
            for b in range(3):
                raw = [F[step, pop(a, b, e), rows, :] for e in range(3)]
                moved = pltpu.roll(jnp.where(lane == 0, raw[2], raw[1]), 2 * b + 1, 1)
                packed = moved if b == 0 else jnp.where(lane >= 2 * b, moved, packed)
                for e in range(3):
                    xs[step, a - 1, 3 * b + e] = turn(raw[e], e)
            xzs[step, a - 1] = packed
            for i in range(9, 15):
                xs[step, a - 1, i] = F[step, first + i, rows, :]
        faces = messages_x(step)
        for copy in faces:
            copy.start()

    def send_y(step):
        for b in SIDES:
            row = block(1) + (7 if b == 1 else 0)
            packed = None
            for a in range(3):
                raw = [F[step, pop(a, b, e), pl.ds(row, 8, stride=16), :] for e in range(3)]
                moved = pltpu.roll(jnp.where(lane == 0, raw[2], raw[1]), 2 * a + 1, 1)
                packed = moved if a == 0 else jnp.where(lane >= 2 * a, moved, packed)
                for e in range(3):
                    ys[step, b - 1, 3 * a + e] = turn(raw[e], e)
            yzs[step, b - 1] = packed
            for j in range(6):
                ys[step, b - 1, 9 + j] = F[step, SOOT[1, b] + j, pl.ds(row, 8, stride=16), :]
        for copy in messages_y(step):
            copy.start()

    def fix_z(step):
        message_z(step).wait()
        plus, minus = zh[step, 0], pltpu.roll(zh[step, 1], 126, 1)

        def fix_layers(i, carry):
            for x in (2 * i, 2 * i + 1):
                rows = pl.ds(pl.multiple_of(16 * x + 24, 8), 8)
                packed = jnp.where(lane & 7 == x, plus, minus)
                for place in range(15):
                    moved = pltpu.roll(packed, (128 - 8 * place - x) & 127, 1)
                    for e, field in zip(SIDES, z_fields(place)):
                        pltpu.store(F.at[step, field, rows, :], moved, mask=lane == lane_of(e))
            return carry

        lax.fori_loop(0, 4, fix_layers, 0)

    def unpacked(packed, i, e):
        shift = (128 - 2 * i - (0 if e == 1 else 2)) % 128
        return pltpu.roll(packed, shift, 1) if shift else packed

    def fix_y(step):
        for copy in messages_y(step):
            copy.wait()
        for b in SIDES:
            row = block(1) + (-1 if b == 1 else 8)
            for a in range(3):
                for e in range(3):
                    value = yh[step, b - 1, 3 * a + e]
                    if e:
                        value = jnp.where(lane == lane_of(e), unpacked(yzh[step, b - 1], a, e), value)
                    F[step, pop(a, b, e), pl.ds(row, 8, stride=16), :] = value
            for j in range(6):
                F[step, SOOT[1, b] + j, pl.ds(row, 8, stride=16), :] = yh[step, b - 1, 9 + j]

    def fix_x(step):
        for copy in messages_x(step):
            copy.wait()
        for a in SIDES:
            slot = 0 if a == 1 else 9
            packed = xzh[step, a - 1]
            for b in range(3):
                for e in SIDES:
                    moved = unpacked(packed, b, e)
                    there = F.at[step, pop(a, b, e), block(slot) : block(slot) + 8, :]
                    pltpu.store(there, moved, mask=lane == lane_of(e))

    def fix_xy(step):
        far = messages_xy(step)
        for copy in far[4:] + far[:4]:
            copy.wait()
        other = ((sublane == 1) & (lane == 0)) | ((sublane == 2) & (lane == LAST))
        for d, (a, b) in enumerate(CORNERS):
            x, row = 0 if a == 1 else 7, 0 if b == 1 else 7
            value = jnp.where(other, xyzh[step, d], xyh[step, d])
            for e in range(3):
                pops[9 * a + 3 * b + e, x, row : row + 1, :] = value[e : e + 1, :]

    for load in loads:
        load.wait()
    moment_constants(rates, consts)

    def one_pass(step, carry):
        @pl.when(step > 0)
        def _():
            fix_z(step - 1)
            fix_y(step - 1)

        def two_layers(i, carry):
            i = lax.rem(i + jnp.where(step == STEPS, 1, 0), 4)
            layers = (jnp.where(i == 0, 0, 2 * i - 1), jnp.where(i == 0, 7, 2 * i))

            @pl.when((step > 0) & (i == 0))
            def _():
                fix_x(step - 1)

            @pl.when(step > 0)
            def _():
                for x in layers:
                    pull(step - 1, x, F, C, pops, soot)

            @pl.when((step > 0) & (i == 0))
            def _():
                fix_xy(step - 1)

            @pl.when(step < STEPS)
            def _():
                for x in layers:
                    layer_out(step, x, pops, consts, F, U)

            @pl.when((step < STEPS) & (i == 0))
            def _():
                send_edges(step)

            @pl.when(step < STEPS)
            def _():
                for x in layers:
                    soot_out(step, x, soot, R, F, C, U)

            @pl.when((step < STEPS) & (i == 0))
            def _():
                send_x(step)

            return carry

        lax.fori_loop(0, 4, two_layers, 0)

        @pl.when(step < STEPS)
        def _():
            send_y(step)

            def turn_layers(i, carry):
                for x in (2 * i, 2 * i + 1):
                    turn_layer(step, x, F, zs)
                return carry

            lax.fori_loop(0, 4, turn_layers, 0)
            message_z(step).start()

        return carry

    lax.fori_loop(0, STEPS + 1, one_pass, 0)


def write_back(pops_ref, soot_ref, pops_out, soot_out, sem):
    copies = [
        pltpu.make_async_copy(pops_ref, pops_out, sem.at[0]),
        pltpu.make_async_copy(soot_ref, soot_out, sem.at[1]),
    ]
    for copy in copies:
        copy.start()
    for copy in copies:
        copy.wait()


def shards(populations, soot_moments, growth_rate, moment_rates):
    f32 = jnp.float32
    hbm = pl.BlockSpec(memory_space=pl.ANY)
    vmem = pl.BlockSpec(memory_space=pltpu.VMEM)
    held = pl.pallas_call(
        kernel,
        out_shape=(pltpu.VMEM(populations.shape, f32), pltpu.VMEM(soot_moments.shape, f32)),
        in_specs=[hbm, hbm, hbm, hbm],
        out_specs=(vmem, vmem),
        scratch_shapes=[
            pltpu.VMEM(growth_rate.shape, f32),
            pltpu.VMEM((STEPS, FIELDS, ROWS, 128), f32),
            pltpu.VMEM(soot_moments.shape, f32),
            pltpu.VMEM((3,) + growth_rate.shape, f32),
            pltpu.VMEM((STEPS, 2, 15, 8, 128), f32),
            pltpu.VMEM((STEPS, 2, 8, 128), f32),
            pltpu.VMEM((STEPS, 2, 8, 128), f32),
            pltpu.VMEM((STEPS, 4, 8, 128), f32),
            pltpu.VMEM((STEPS, 4, 8, 128), f32),
            pltpu.VMEM((STEPS, 4, 8, 128), f32),
            pltpu.VMEM((STEPS, 2, 15, 8, 128), f32),
            pltpu.VMEM((STEPS, 2, 15, 8, 128), f32),
            pltpu.VMEM((STEPS, 2, 8, 128), f32),
            pltpu.VMEM((STEPS, 2, 8, 128), f32),
            pltpu.VMEM((STEPS, 2, 8, 128), f32),
            pltpu.VMEM((STEPS, 2, 8, 128), f32),
            pltpu.SMEM((27,), f32),
            pltpu.SMEM((54,), f32),
            pltpu.SemaphoreType.DMA((4,)),
            pltpu.SemaphoreType.DMA((STEPS, MESSAGES)),
            pltpu.SemaphoreType.DMA((STEPS, MESSAGES)),
        ],
        compiler_params=pltpu.CompilerParams(
            collective_id=0, has_side_effects=True
        ),
    )(populations, soot_moments, growth_rate, moment_rates)
    anywhere = pl.BlockSpec(memory_space=pl.ANY)
    return pl.pallas_call(
        write_back,
        out_shape=tuple(jax.ShapeDtypeStruct(a.shape, f32) for a in held),
        in_specs=[anywhere] * 2,
        out_specs=(pl.BlockSpec(memory_space=pltpu.HBM),) * 2,
        scratch_shapes=[pltpu.SemaphoreType.DMA((2,))],
        compiler_params=pltpu.CompilerParams(vmem_limit_bytes=1024 * 1024),
    )(*held)


def solution(mesh):
    in_specs = (P(None, "gx", "gy", "gz"), P(None, "gx", "gy", "gz"), P("gx", "gy", "gz"), P())
    out_specs = (P(None, "gx", "gy", "gz"), P(None, "gx", "gy", "gz"))
    return jax.shard_map(shards, mesh=mesh, in_specs=in_specs, out_specs=out_specs, check_vma=False)
```

```python
import functools

import jax
import jax.numpy as jnp
from jax import lax
from jax.experimental import pallas as pl
from jax.experimental.pallas import tpu as pltpu
from jax.sharding import PartitionSpec as P

MESH = pl.DeviceIdType.MESH
STEPS = 2
KAPPA = (0.08, 0.06, 0.05, 0.04, 0.035, 0.03)
SPEED = (0, 1, -1)
LAST = 127
SIDES = (1, 2)
CORNERS = ((1, 1), (1, 2), (2, 1), (2, 2))
SOOT = {(0, 1): 18, (0, 2): 33, (1, 1): 39, (1, 2): 45, (2, 1): 51, (2, 2): 57}
FIELDS = 63
ROWS = 168
X, XZ, XY, XYZ, Y, YZ, Z = 0, 2, 4, 8, 12, 14, 16
MESSAGES = 17


def pop(a, b, e):
    return (0, 9, 24)[a] + 3 * b + e


def block(slot):
    return 16 * slot + 8


def forward(f):
    total = f[1] + f[2]
    return (4.0 * f[0] + total, f[1] - f[2], total)


def backward(n):
    return (0.5 * (n[0] - n[2]), n[1] + n[2], n[2] - n[1])


def along(values, axis, change):
    out = {}
    for i in range(3):
        for j in range(3):
            keys = [(i, j)[:axis] + (k,) + (i, j)[axis:] for k in range(3)]
            for key, value in zip(keys, change([values[key] for key in keys])):
                out[key] = value
    return out


def moment_constants(rates_ref, consts):
    for index in range(27):
        powers = (index // 9, index // 3 % 3, index % 3)
        rate = rates_ref[index]
        consts[index] = 0.125 - 0.125 * rate
        consts[27 + index] = rate * (27.0 / 3.0 ** powers.count(2))


def collide(g, consts):
    m = g
    for axis in (2, 1, 0):
        m = along(m, axis, forward)
    scale = 1.0 / 216.0
    density = m[0, 0, 0] * scale
    u = (m[1, 0, 0] * scale, m[0, 1, 0] * scale, m[0, 0, 1] * scale)
    square = [3.0 * v * v for v in u]
    product = {(0, 1): u[0] * u[1], (0, 2): u[0] * u[2], (1, 2): u[1] * u[2]}
    n = {}
    for key, value in m.items():
        index = 9 * key[0] + 3 * key[1] + key[2]
        odd = tuple(i for i in range(3) if key[i] == 1)
        part = consts[index] * value
        if len(odd) == 3:
            n[key] = part
            continue
        if len(odd) == 0:
            balance = density
            for i in range(3):
                if key[i] == 2:
                    balance = balance + square[i]
        elif len(odd) == 1:
            balance = u[odd[0]]
        else:
            balance = product[odd]
        n[key] = part + consts[27 + index] * balance
    for axis in (0, 1, 2):
        n = along(n, axis, backward)
    return n, u


def turn(value, e):
    return value if e == 0 else pltpu.roll(value, 1 if e == 1 else LAST, 1)


def lane_of(e):
    return 0 if e == 1 else LAST


def both(lane, one, two):
    return jnp.where(lane == LAST, two, one)


def z_fields(place):
    if place < 9:
        return tuple(pop(place // 3, place % 3, e) for e in SIDES)
    return tuple(SOOT[2, e] + place - 9 for e in SIDES)


def layer_out(step, x, pops, consts, F, U):
    rows = pl.ds(pl.multiple_of(16 * x + 24, 8), 8)
    g = {(k // 9, k // 3 % 3, k % 3): pops[k, x] for k in range(27)}
    n, u = collide(g, consts)
    for (a, b, e), value in n.items():
        F[step, pop(a, b, e), rows, :] = value
    for axis in range(3):
        U[axis, x] = u[axis]


def soot_out(step, x, soot_ref, growth, F, center, U):
    rows = pl.ds(pl.multiple_of(16 * x + 24, 8), 8)
    half = [0.5 * U[axis, x] for axis in range(3)]
    for j in range(6):
        soot = soot_ref[j, x]
        for axis in range(3):
            F[step, SOOT[axis, 1] + j, rows, :] = soot * (KAPPA[j] + half[axis])
            F[step, SOOT[axis, 2] + j, rows, :] = soot * (KAPPA[j] - half[axis])
        center[j, x] = soot * (growth[x] + (1.0 - 6.0 * KAPPA[j]))


def turn_layer(step, x, F, zs):
    lane = lax.broadcasted_iota(jnp.int32, (8, 128), 1)
    rows = pl.ds(pl.multiple_of(16 * x + 24, 8), 8)
    past = lane - x
    packed = None
    for place in range(15):
        one, two = z_fields(place)
        plus, minus = F[step, one, rows, :], F[step, two, rows, :]
        F[step, one, rows, :] = turn(plus, 1)
        F[step, two, rows, :] = turn(minus, 2)
        moved = pltpu.roll(jnp.where(lane == 0, minus, plus), 8 * place + 1 + x, 1)
        packed = moved if place == 0 else jnp.where(past >= 8 * place, moved, packed)
    left = lane & 7
    zs[step, 0] = jnp.where(left == x, packed, zs[step, 0])
    zs[step, 1] = jnp.where(left == ((x + 1) & 7), packed, zs[step, 1])


def pull(step, x, F, center, pops, soot_ref):
    for a in range(3):
        for b in range(3):
            for e in range(3):
                pops[9 * a + 3 * b + e, x] = F[step, pop(a, b, e), pl.ds(16 * (x - SPEED[a]) + 24 - SPEED[b], 8), :]
    for j in range(6):
        total = center[j, x]
        for axis in range(3):
            for side in SIDES:
                move = (16, 1, 0)[axis] * SPEED[side]
                total = total + F[step, SOOT[axis, side] + j, pl.ds(16 * x + 24 - move, 8), :]
        soot_ref[j, x] = total


def kernel(
    pops_ref, soot_ref, growth_ref, rates_ref, pops, soot,
    R, F, C, U, xs, xzs, xzh, xys, xyh, xyzh, ys, yh, yzs, yzh, zs, zh, rates, consts, load_sem, send_sem, recv_sem,
):
    position = tuple(lax.axis_index(axis) for axis in ("gx", "gy", "gz"))
    counts = tuple(lax.axis_size(axis) for axis in ("gx", "gy", "gz"))

    near = [{0: p, 1: lax.rem(p + 1, n), -1: lax.rem(p + (n - 1), n)} for p, n in zip(position, counts)]

    def device(*move):
        return tuple(at[m] for at, m in zip(near, move))

    targets = [(i, j, k) for i in (0, 1, -1) for j in (0, 1, -1) for k in (0, 1) if (i, j, k) != (0, 0, 0)]
    barrier = pltpu.get_barrier_semaphore()
    for target in sorted(targets, key=lambda t: (-abs(t[0]) - abs(t[1]), t[2])):
        pl.semaphore_signal(barrier, inc=1, device_id=device(*target), device_id_type=MESH)

    loads = [
        pltpu.make_async_copy(source, target, load_sem.at[i])
        for i, (source, target) in enumerate([(rates_ref, rates), (pops_ref, pops), (soot_ref, soot), (growth_ref, R)])
    ]
    for load in loads:
        load.start()
    zs[...] = jnp.zeros_like(zs)
    xys[...] = jnp.zeros_like(xys)

    lane = lax.broadcasted_iota(jnp.int32, (8, 128), 1)
    sublane = lax.broadcasted_iota(jnp.int32, (8, 128), 0)

    def message(step, index, source, target, move):
        return pltpu.make_async_remote_copy(
            src_ref=source,
            dst_ref=target,
            send_sem=send_sem.at[step, index],
            recv_sem=recv_sem.at[step, index],
            device_id=device(*move),
            device_id_type=MESH,
        )

    def messages_xy(step):
        out = []
        for d, (a, b) in enumerate(CORNERS):
            out.append(message(step, XY + d, xys.at[step, d], xyh.at[step, d], (SPEED[a], SPEED[b], 0)))
        for d, (a, b) in enumerate(CORNERS):
            out.append(message(step, XYZ + d, xys.at[step, d], xyzh.at[step, d], (SPEED[a], SPEED[b], 1)))
        return out

    def messages_x(step):
        out = []
        for a in SIDES:
            first, slot = (9, 0) if a == 1 else (24, 9)
            there = F.at[step, pl.ds(first, 15), pl.ds(block(slot), 8)]
            out.append(message(step, X + a - 1, xs.at[step, a - 1], there, (SPEED[a], 0, 0)))
        for a in SIDES:
            out.append(message(step, XZ + a - 1, xzs.at[step, a - 1], xzh.at[step, a - 1], (SPEED[a], 0, 1)))
        return out

    def messages_y(step):
        out = []
        for b in SIDES:
            out.append(message(step, Y + b - 1, ys.at[step, b - 1], yh.at[step, b - 1], (0, SPEED[b], 0)))
        for b in SIDES:
            out.append(message(step, YZ + b - 1, yzs.at[step, b - 1], yzh.at[step, b - 1], (0, SPEED[b], 1)))
        return out

    def message_z(step):
        return message(step, Z, zs.at[step], zh.at[step], (0, 0, 1))

    def send_edges(step):
        for d, (a, b) in enumerate(CORNERS):
            first = block(8 if a == 1 else 1)
            row = 7 if b == 1 else 0
            for e in range(3):
                value = turn(F[step, pop(a, b, e), first : first + 8, :], e)
                xys[step, d, e : e + 1, :] = value[row : row + 1, :]

        @pl.when(step == 0)
        def _():
            pl.semaphore_wait(barrier, len(targets))

        for copy in messages_xy(step):
            copy.start()

    def send_x(step):
        for a in SIDES:
            first, rows = (9, slice(block(8), block(8) + 8)) if a == 1 else (24, slice(block(1), block(1) + 8))
            packed = None
            for b in range(3):
                raw = [F[step, pop(a, b, e), rows, :] for e in range(3)]
                moved = pltpu.roll(jnp.where(lane == 0, raw[2], raw[1]), 2 * b + 1, 1)
                packed = moved if b == 0 else jnp.where(lane >= 2 * b, moved, packed)
                for e in range(3):
                    xs[step, a - 1, 3 * b + e] = turn(raw[e], e)
            xzs[step, a - 1] = packed
            for i in range(9, 15):
                xs[step, a - 1, i] = F[step, first + i, rows, :]
        faces = messages_x(step)
        for copy in faces:
            copy.start()

    def send_y(step):
        for b in SIDES:
            row = block(1) + (7 if b == 1 else 0)
            packed = None
            for a in range(3):
                raw = [F[step, pop(a, b, e), pl.ds(row, 8, stride=16), :] for e in range(3)]
                moved = pltpu.roll(jnp.where(lane == 0, raw[2], raw[1]), 2 * a + 1, 1)
                packed = moved if a == 0 else jnp.where(lane >= 2 * a, moved, packed)
                for e in range(3):
                    ys[step, b - 1, 3 * a + e] = turn(raw[e], e)
            yzs[step, b - 1] = packed
            for j in range(6):
                ys[step, b - 1, 9 + j] = F[step, SOOT[1, b] + j, pl.ds(row, 8, stride=16), :]
        for copy in messages_y(step):
            copy.start()

    def fix_z(step):
        message_z(step).wait()
        plus, minus = zh[step, 0], pltpu.roll(zh[step, 1], 126, 1)

        def fix_layers(i, carry):
            for x in (2 * i, 2 * i + 1):
                rows = pl.ds(pl.multiple_of(16 * x + 24, 8), 8)
                packed = jnp.where(lane & 7 == x, plus, minus)
                for place in range(15):
                    moved = pltpu.roll(packed, (128 - 8 * place - x) & 127, 1)
                    for e, field in zip(SIDES, z_fields(place)):
                        pltpu.store(F.at[step, field, rows, :], moved, mask=lane == lane_of(e))
            return carry

        lax.fori_loop(0, 4, fix_layers, 0)

    def unpacked(packed, i, e):
        shift = (128 - 2 * i - (0 if e == 1 else 2)) % 128
        return pltpu.roll(packed, shift, 1) if shift else packed

    def fix_y(step):
        for copy in messages_y(step):
            copy.wait()
        for b in SIDES:
            row = block(1) + (-1 if b == 1 else 8)
            for a in range(3):
                for e in range(3):
                    value = yh[step, b - 1, 3 * a + e]
                    if e:
                        value = jnp.where(lane == lane_of(e), unpacked(yzh[step, b - 1], a, e), value)
                    F[step, pop(a, b, e), pl.ds(row, 8, stride=16), :] = value
            for j in range(6):
                F[step, SOOT[1, b] + j, pl.ds(row, 8, stride=16), :] = yh[step, b - 1, 9 + j]

    def fix_x(step):
        for copy in messages_x(step):
            copy.wait()
        for a in SIDES:
            slot = 0 if a == 1 else 9
            packed = xzh[step, a - 1]
            for b in range(3):
                for e in SIDES:
                    moved = unpacked(packed, b, e)
                    there = F.at[step, pop(a, b, e), block(slot) : block(slot) + 8, :]
                    pltpu.store(there, moved, mask=lane == lane_of(e))

    def fix_xy(step):
        far = messages_xy(step)
        for copy in far[4:] + far[:4]:
            copy.wait()
        other = ((sublane == 1) & (lane == 0)) | ((sublane == 2) & (lane == LAST))
        for d, (a, b) in enumerate(CORNERS):
            x, row = 0 if a == 1 else 7, 0 if b == 1 else 7
            value = jnp.where(other, xyzh[step, d], xyh[step, d])
            for e in range(3):
                pops[9 * a + 3 * b + e, x, row : row + 1, :] = value[e : e + 1, :]

    for load in loads:
        load.wait()
    moment_constants(rates, consts)

    def one_pass(step, carry):
        @pl.when(step > 0)
        def _():
            fix_z(step - 1)
            fix_y(step - 1)

        def two_layers(i, carry):
            i = lax.rem(i + jnp.where(step == STEPS, 1, 0), 4)
            layers = (jnp.where(i == 0, 0, 2 * i - 1), jnp.where(i == 0, 7, 2 * i))

            @pl.when((step > 0) & (i == 0))
            def _():
                fix_x(step - 1)

            @pl.when(step > 0)
            def _():
                for x in layers:
                    pull(step - 1, x, F, C, pops, soot)

            @pl.when((step > 0) & (i == 0))
            def _():
                fix_xy(step - 1)

            @pl.when(step < STEPS)
            def _():
                for x in layers:
                    layer_out(step, x, pops, consts, F, U)

            @pl.when((step < STEPS) & (i == 0))
            def _():
                send_edges(step)

            @pl.when(step < STEPS)
            def _():
                for x in layers:
                    soot_out(step, x, soot, R, F, C, U)

            @pl.when((step < STEPS) & (i == 0))
            def _():
                send_x(step)

            return carry

        lax.fori_loop(0, 4, two_layers, 0)

        @pl.when(step < STEPS)
        def _():
            send_y(step)

            def turn_layers(i, carry):
                for x in (2 * i, 2 * i + 1):
                    turn_layer(step, x, F, zs)
                return carry

            lax.fori_loop(0, 4, turn_layers, 0)
            message_z(step).start()

        return carry

    lax.fori_loop(0, STEPS + 1, one_pass, 0)


def write_back(pops_ref, soot_ref, pops_out, soot_out, sem):
    copies = [
        pltpu.make_async_copy(pops_ref, pops_out, sem.at[0]),
        pltpu.make_async_copy(soot_ref, soot_out, sem.at[1]),
    ]
    for copy in copies:
        copy.start()
    for copy in copies:
        copy.wait()


def shards(populations, soot_moments, growth_rate, moment_rates):
    f32 = jnp.float32
    hbm = pl.BlockSpec(memory_space=pl.ANY)
    vmem = pl.BlockSpec(memory_space=pltpu.VMEM)
    held = pl.pallas_call(
        kernel,
        out_shape=(pltpu.VMEM(populations.shape, f32), pltpu.VMEM(soot_moments.shape, f32)),
        in_specs=[hbm, hbm, hbm, hbm],
        out_specs=(vmem, vmem),
        scratch_shapes=[
            pltpu.VMEM(growth_rate.shape, f32),
            pltpu.VMEM((STEPS, FIELDS, ROWS, 128), f32),
            pltpu.VMEM(soot_moments.shape, f32),
            pltpu.VMEM((3,) + growth_rate.shape, f32),
            pltpu.VMEM((STEPS, 2, 15, 8, 128), f32),
            pltpu.VMEM((STEPS, 2, 8, 128), f32),
            pltpu.VMEM((STEPS, 2, 8, 128), f32),
            pltpu.VMEM((STEPS, 4, 8, 128), f32),
            pltpu.VMEM((STEPS, 4, 8, 128), f32),
            pltpu.VMEM((STEPS, 4, 8, 128), f32),
            pltpu.VMEM((STEPS, 2, 15, 8, 128), f32),
            pltpu.VMEM((STEPS, 2, 15, 8, 128), f32),
            pltpu.VMEM((STEPS, 2, 8, 128), f32),
            pltpu.VMEM((STEPS, 2, 8, 128), f32),
            pltpu.VMEM((STEPS, 2, 8, 128), f32),
            pltpu.VMEM((STEPS, 2, 8, 128), f32),
            pltpu.SMEM((27,), f32),
            pltpu.SMEM((54,), f32),
            pltpu.SemaphoreType.DMA((4,)),
            pltpu.SemaphoreType.DMA((STEPS, MESSAGES)),
            pltpu.SemaphoreType.DMA((STEPS, MESSAGES)),
        ],
        compiler_params=pltpu.CompilerParams(
            collective_id=0, has_side_effects=True
        ),
    )(populations, soot_moments, growth_rate, moment_rates)
    anywhere = pl.BlockSpec(memory_space=pl.ANY)
    return pl.pallas_call(
        write_back,
        out_shape=tuple(jax.ShapeDtypeStruct(a.shape, f32) for a in held),
        in_specs=[anywhere] * 2,
        out_specs=(pl.BlockSpec(memory_space=pltpu.HBM),) * 2,
        scratch_shapes=[pltpu.SemaphoreType.DMA((2,))],
        compiler_params=pltpu.CompilerParams(vmem_limit_bytes=1024 * 1024),
    )(*held)


def solution(mesh):
    in_specs = (P(None, "gx", "gy", "gz"), P(None, "gx", "gy", "gz"), P("gx", "gy", "gz"), P())
    out_specs = (P(None, "gx", "gy", "gz"), P(None, "gx", "gy", "gz"))
    return jax.shard_map(shards, mesh=mesh, in_specs=in_specs, out_specs=out_specs, check_vma=False)
```
